512 devices in a mesh: rep: 16 (over x, z_hi), feat: 32 (over z_lo, y, core).
Axes of the slice: x: 4, y: 8, z: 8 (z_hi: 4, z_lo: 2; z = z_hi * 2 + z_lo), core: 2. Of those that a mesh axis runs over, the one named last changes fastest.
Arguments:
- basis: float32 [16, 64, 131072], P('rep', None, 'feat'), may hold values from -6 to 6
- stream: bfloat16 [16, 2, 128, 131072], P('rep', None, None, 'feat'), may hold values from -6 to 6
Outputs:
- new_basis: float32 [16, 64, 131072], P('rep', None, 'feat')
The draws below stay inside these ranges and needn't reach their ends.
All inputs are finite; a program needn't handle non-finite values.
Results may differ from the reference program's by a relative error of at most 0.0003.
Values sent between devices are 32-bit elements; how exact they have to be, the bound alone decides.
No kernel may reach another device: no remote copies, remote signals or barrier semaphores. Data moves between devices by JAX's collectives and lax.ppermute only.
A program may use at most 64 MiB of HBM per device.

```python
import jax
import jax.numpy as jnp
from jax import lax

RANK = 64
BATCH = 128
STEPS = 2
NF = 131072
REPS = 16


def draw_basis(key, part):
    shape = (REPS, RANK, NF)
    inner = jax.random.fold_in(key, 11)
    values = jax.random.normal(inner, shape, jnp.float32)
    return jnp.clip(values, -6.0, 6.0)


def draw_stream(key, part):
    shape = (REPS, STEPS, BATCH, NF)
    inner = jax.random.fold_in(key, 21)
    values = jax.random.normal(inner, shape, jnp.float32)
    return jnp.clip(values, -6.0, 6.0).astype(jnp.bfloat16)


def setup_inputs(seed: int = 0) -> dict:
    arg_keys = jax.random.split(jax.random.key(seed), 3)
    return {
        "basis": draw_basis(jax.random.fold_in(arg_keys[2], 71), 0),
        "stream": draw_stream(jax.random.fold_in(arg_keys[2], 71), 0),
    }


learn_rate = 0.5

def one_replica(pair):
    start, batches, average = pair
    scale = jnp.sqrt(jnp.float32(NF))
    step_size = learn_rate / BATCH
    current = start
    for step in range(STEPS):
        rows = batches[step].astype(jnp.float32)
        proj = jnp.dot(rows.astype(jnp.float32), current.T.astype(jnp.float32), precision=lax.Precision.HIGHEST, preferred_element_type=jnp.float32) / scale
        cov = jnp.dot(proj.T.astype(jnp.float32), proj.astype(jnp.float32), precision=lax.Precision.HIGHEST, preferred_element_type=jnp.float32)
        drive = jnp.dot(proj.T.astype(jnp.float32), rows.astype(jnp.float32), precision=lax.Precision.HIGHEST, preferred_element_type=jnp.float32)
        shrink = jnp.dot(cov.astype(jnp.float32), current.astype(jnp.float32), precision=lax.Precision.HIGHEST, preferred_element_type=jnp.float32)
        current = current + step_size * (drive - shrink)
    mixed = current + average - start
    gram = jnp.dot(mixed.astype(jnp.float32), mixed.T.astype(jnp.float32), precision=lax.Precision.HIGHEST, preferred_element_type=jnp.float32) / NF
    lower = jnp.linalg.cholesky(gram)
    return lax.linalg.triangular_solve(lower, mixed, left_side=True, lower=True)

def reference(basis, stream):
    average = lax.optimization_barrier(jnp.sum(basis, axis=0)) / REPS

    def apply_one(pair):
        return one_replica((pair[0], pair[1], average))
    return lax.map(apply_one, (basis, stream))
```

```python
import jax
import jax.numpy as jnp
from jax import lax
from jax.experimental import pallas as pl
from jax.experimental.pallas import tpu as pltpu
from jax.sharding import Mesh, PartitionSpec as P

REP = ("x", "zh")
FEAT = ("zl", "y", "core")
AXES = REP + FEAT
SIZES = (4, 4, 2, 8, 2)
LEARN_RATE = 0.5
HIGHEST = lax.Precision.HIGHEST


def dot(left, right, dims):
    return lax.dot_general(
        left, right, (dims, ((), ())), precision=HIGHEST, preferred_element_type=jnp.float32
    )


def spread(value, axis, parts):
    return lax.all_to_all(jnp.broadcast_to(value, (parts,) + value.shape), axis, 0, 0)


def replica_average(start):
    rank, width = start.shape
    part = lax.all_to_all(start.reshape(4, rank // 4, width), "x", 0, 0).sum(0)
    part = lax.all_to_all(part.reshape(4, rank // 16, width), "zh", 0, 0).sum(0)
    part = spread(part * (1.0 / 16.0), "zh", 4).reshape(rank // 4, width)
    return spread(part, "x", 4).reshape(rank, width)


def feature_sum(value):
    part = lax.all_to_all(value.reshape(32, 8, 128), FEAT, 0, 0).sum(0)
    return spread(part, FEAT, 32).reshape(256, 128)


def finish_kernel(parts_ref, mixed_ref, out_ref, *, total_feat):
    packed = parts_ref[0]
    for index in range(1, parts_ref.shape[0]):
        packed = packed + parts_ref[index]
    packed = packed / total_feat
    gram = jnp.concatenate([packed[:, :64], packed[:, 64:]], axis=0)
    lanes = lax.broadcasted_iota(jnp.int32, (8, 128), 1)
    subs = lax.broadcasted_iota(jnp.int32, (8, 128), 0)
    blocks = []
    for b in range(8):
        eye = jnp.where(lanes == subs + (64 + 8 * b), 1.0, 0.0).astype(jnp.float32)
        left = jnp.concatenate([gram[8 * b : 8 * b + 8], jnp.zeros((8, 64), jnp.float32)], axis=1)
        blocks.append(left + eye)
    done = []
    for k in range(64):
        home, sub = divmod(k, 8)
        row = blocks[home][sub : sub + 1, :]
        pivot = row[:, k : k + 1]
        scaled = row / pivot
        for b in range(home, 8):
            col = blocks[b][:, k : k + 1]
            if b == home:
                col = jnp.where(subs[:, :1] > sub, col, 0.0)
            blocks[b] = blocks[b] - col * scaled
        done.append(row[:, 64:] * lax.rsqrt(pivot))
    inverse = jnp.concatenate(done, axis=0)
    out_ref[...] = jnp.dot(
        inverse, mixed_ref[...], precision=HIGHEST, preferred_element_type=jnp.float32
    )


def finish(parts, mixed, total_feat):
    import functools

    return pl.pallas_call(
        functools.partial(finish_kernel, total_feat=total_feat),
        out_shape=jax.ShapeDtypeStruct(mixed.shape, jnp.float32),
        in_specs=[pl.BlockSpec(memory_space=pltpu.VMEM)] * 2,
        out_specs=pl.BlockSpec(memory_space=pltpu.VMEM),
        compiler_params=pltpu.CompilerParams(vmem_limit_bytes=32 * 1024 * 1024),
    )(parts, mixed)


def per_device(basis, stream):
    start = basis[0]
    rows0, rows1 = stream[0, 0], stream[0, 1]
    rank = start.shape[0]
    total_feat = start.shape[1] * 32
    inv_scale = 1.0 / jnp.sqrt(jnp.float32(total_feat))
    step_size = LEARN_RATE / rows0.shape[0]

    on_cols = ((1,), (1,))
    start_t = dot(stream[0].reshape(256, -1), start, on_cols)
    cross = dot(rows1, rows0, on_cols)
    packed = jnp.concatenate([jnp.concatenate([start_t[:128], start_t[128:]], axis=1), cross], axis=0)
    average = replica_average(start)
    packed = feature_sum(packed)

    eye = jnp.eye(rank, dtype=jnp.float32)
    on_rows = ((0,), (0,))
    plain = ((1,), (0,))
    proj0 = packed[:128, :64] * inv_scale
    cov0 = dot(proj0, proj0, on_rows)
    keep0 = eye - step_size * cov0
    proj1 = (dot(packed[:128, 64:], keep0, plain) + step_size * dot(packed[128:], proj0, plain)) * inv_scale
    cov1 = dot(proj1, proj1, on_rows)
    mix_b = step_size * (step_size * dot(cov1, cov0, plain) - cov0 - cov1)
    mix_0 = step_size * (proj0.T - step_size * dot(cov1, proj0, ((1,), (1,))))
    mix_1 = step_size * proj1.T
    delta = dot(mix_b, start, plain) + dot(mix_0, rows0, plain) + dot(mix_1, rows1, plain)

    mixed = average + delta
    gram = dot(mixed, mixed, on_cols)
    gram = jnp.concatenate([gram[:32], gram[32:]], axis=1)
    gram = gram + lax.ppermute(gram, "core", [(0, 1), (1, 0)])
    parts = spread(gram, ("zl", "y"), 16)
    return finish(parts, mixed, float(total_feat))[None]


def solution(mesh):
    fine = Mesh(mesh.devices.reshape(SIZES), AXES)
    placed = (P(REP, None, FEAT), P(REP, None, None, FEAT))
    return jax.shard_map(
        per_device, mesh=fine, in_specs=placed, out_specs=P(REP, None, FEAT), check_vma=False
    )
```

```python
import functools

import jax
import jax.numpy as jnp
from jax import lax
from jax.experimental import pallas as pl
from jax.experimental.pallas import tpu as pltpu
from jax.sharding import Mesh, PartitionSpec as P

REP = ("x", "zh")
FEAT = ("zl", "y", "core")
AXES = REP + FEAT
SIZES = (4, 4, 2, 8, 2)
LEARN_RATE = 0.5
HIGHEST = lax.Precision.HIGHEST
SWAP = [(0, 1), (1, 0)]
PLAIN = ((1,), (0,))
ON_ROWS = ((0,), (0,))
ON_COLS = ((1,), (1,))


def dot(left, right, dims, precision=HIGHEST):
    return lax.dot_general(
        left, right, (dims, ((), ())), precision=precision, preferred_element_type=jnp.float32
    )


def split3(value):
    high = value.astype(jnp.bfloat16)
    rest = value - high.astype(jnp.float32)
    middle = rest.astype(jnp.bfloat16)
    low = (rest - middle.astype(jnp.float32)).astype(jnp.bfloat16)
    return high, middle, low


def kernel_call(body, shapes, args, flops, moved):
    return pl.pallas_call(
        body,
        out_shape=shapes,
        in_specs=[pl.BlockSpec(memory_space=pltpu.VMEM)] * len(args),
        out_specs=jax.tree.map(lambda _: pl.BlockSpec(memory_space=pltpu.VMEM), shapes),
        cost_estimate=pl.CostEstimate(flops=flops, bytes_accessed=moved, transcendentals=0),
        compiler_params=pltpu.CompilerParams(vmem_limit_bytes=40 * 1024 * 1024),
    )(*args)


def f32(*shape):
    return jax.ShapeDtypeStruct(shape, jnp.float32)


def products_kernel(start_ref, stream_ref, out_ref):
    rows = jnp.concatenate([stream_ref[0], stream_ref[1]], axis=0)
    right = jnp.concatenate(split3(start_ref[...]) + (stream_ref[0],), axis=0)
    both = dot(rows, right, ON_COLS, None)
    onto = both[:, :64] + (both[:, 64:128] + both[:, 128:192])
    out_ref[:128] = jnp.concatenate([onto[:128], onto[128:]], axis=1)
    out_ref[128:] = both[128:, 192:]


def pack_kernel(received_ref, feat_ref, other_ref, out_ref):
    for piece in range(32):
        cols = slice(128 * piece, 128 * piece + 128)
        out_ref[piece, :16] = (received_ref[0, :, cols] + received_ref[1, :, cols]) + (
            received_ref[2, :, cols] + received_ref[3, :, cols]
        )
        rows = slice(8 * piece, 8 * piece + 8)
        out_ref[piece, 16:] = feat_ref[rows] + other_ref[rows]


def turn_kernel(received_ref, out_ref):
    for y in range(8):
        part = (received_ref[y, :16] + received_ref[8 + y, :16]) + (
            received_ref[16 + y, :16] + received_ref[24 + y, :16]
        )
        part = part * (1.0 / 16.0)
        for zh in range(4):
            out_ref[8 * zh + y, :16] = part
    for zh in range(4):
        part = received_ref[8 * zh, 16:]
        for y in range(1, 8):
            part = part + received_ref[8 * zh + y, 16:]
        for y in range(8):
            out_ref[8 * zh + y, 16:] = part


def unpack_kernel(received_ref, chunk_ref, feat_ref):
    for piece in range(32):
        part = received_ref[piece, :16]
        for x in range(4):
            chunk_ref[x, :, 128 * piece : 128 * piece + 128] = part
        feat_ref[8 * piece : 8 * piece + 8] = received_ref[piece, 16:]


def delta_kernel(packed_ref, start_ref, stream_ref, out_ref, *, inv_scale, step_size):
    rank = start_ref.shape[0]
    index = lax.broadcasted_iota(jnp.int32, (rank, rank), 0)
    eye = jnp.where(index == lax.broadcasted_iota(jnp.int32, (rank, rank), 1), 1.0, 0.0)
    onto0 = packed_ref[:128, :64]
    onto1 = packed_ref[:128, 64:]
    cross = packed_ref[128:]
    proj0 = onto0 * inv_scale
    cov0 = dot(proj0, proj0, ON_ROWS)
    proj1 = (dot(onto1, eye - step_size * cov0, PLAIN) + step_size * dot(cross, proj0, PLAIN)) * inv_scale
    cov1 = dot(proj1, proj1, ON_ROWS)
    mix_b = step_size * (step_size * dot(cov1, cov0, PLAIN) - cov0 - cov1)
    turned0 = proj0.T
    mix_0 = step_size * (turned0 - step_size * dot(cov1, turned0, PLAIN))
    mix_1 = step_size * proj1.T
    left = jnp.concatenate(split3(jnp.concatenate([mix_0, mix_1], axis=1)), axis=0)
    rows = jnp.concatenate([stream_ref[0], stream_ref[1]], axis=0)
    three = dot(left, rows, PLAIN, None)
    out_ref[...] = dot(mix_b, start_ref[...], PLAIN) + (
        three[:64] + (three[64:128] + three[128:])
    )


def gram_kernel(average_ref, delta_ref, mixed_ref, gram_ref):
    mixed = average_ref[...] + delta_ref[...]
    mixed_ref[...] = mixed
    stacked = jnp.concatenate(split3(mixed), axis=0)
    both = dot(stacked, stacked, ON_COLS, None)
    high_mid = both[:64, 64:128]
    high_low = both[:64, 128:192]
    small = both[64:128, 64:128] + (high_low + both[128:192, :64])
    gram = both[:64, :64] + ((high_mid + both[64:128, :64]) + small)
    gram_ref[...] = jnp.concatenate([gram[:32], gram[32:]], axis=1)


def finish_kernel(parts_ref, mixed_ref, out_ref, *, total_feat):
    packed = parts_ref[0]
    for index in range(1, parts_ref.shape[0]):
        packed = packed + parts_ref[index]
    packed = packed / total_feat
    gram = jnp.concatenate([packed[:, :64], packed[:, 64:]], axis=0)
    lanes = lax.broadcasted_iota(jnp.int32, (8, 128), 1)
    subs = lax.broadcasted_iota(jnp.int32, (8, 128), 0)
    blocks = []
    for b in range(8):
        eye = jnp.where(lanes == subs + (64 + 8 * b), 1.0, 0.0).astype(jnp.float32)
        left = jnp.concatenate([gram[8 * b : 8 * b + 8], jnp.zeros((8, 64), jnp.float32)], axis=1)
        blocks.append(left + eye)
    done = []
    for k in range(64):
        home, sub = divmod(k, 8)
        row = blocks[home][sub : sub + 1, :]
        pivot = row[:, k : k + 1]
        scaled = row / pivot
        for b in range(home, 8):
            col = blocks[b][:, k : k + 1]
            if b == home:
                col = jnp.where(subs[:, :1] > sub, col, 0.0)
            blocks[b] = blocks[b] - col * scaled
        done.append(row[:, 64:] * lax.rsqrt(pivot))
    inverse = jnp.concatenate(done, axis=0)
    out_ref[...] = dot(inverse, mixed_ref[...], PLAIN)


def per_device(basis, stream):
    start, batches = basis[0], stream[0]
    rank, width = start.shape
    total_feat = float(width * 32)
    mega = 1 << 20

    arrived = lax.all_to_all(start.reshape(4, 16, width), "x", 0, 0)
    feat = kernel_call(products_kernel, f32(256, 128), (start, batches), 700 * mega, 8 * mega)
    feat = feat + lax.ppermute(feat, "core", SWAP)
    other = lax.ppermute(feat, "zl", SWAP)
    packed = kernel_call(pack_kernel, f32(32, 24, 128), (arrived, feat, other), mega, mega)
    packed = lax.all_to_all(packed, ("zh", "y"), 0, 0)
    packed = kernel_call(turn_kernel, f32(32, 24, 128), (packed,), mega, mega)
    packed = lax.all_to_all(packed, ("zh", "y"), 0, 0)
    chunk, feat = kernel_call(
        unpack_kernel, (f32(4, 16, width), f32(256, 128)), (packed,), mega, mega
    )
    average = lax.all_to_all(chunk, "x", 0, 0).reshape(rank, width)
    delta = kernel_call(
        functools.partial(
            delta_kernel, inv_scale=total_feat**-0.5, step_size=LEARN_RATE / batches.shape[1]
        ),
        f32(rank, width),
        (feat, start, batches),
        700 * mega,
        8 * mega,
    )
    mixed, gram = kernel_call(
        gram_kernel, (f32(rank, width), f32(32, 128)), (average, delta), 400 * mega, 3 * mega
    )
    gram = gram + lax.ppermute(gram, "core", SWAP)
    parts = lax.all_to_all(jnp.broadcast_to(gram, (16, 32, 128)), ("zl", "y"), 0, 0)
    return kernel_call(
        functools.partial(finish_kernel, total_feat=total_feat),
        f32(rank, width),
        (parts, mixed),
        400 * mega,
        3 * mega,
    )[None]


def solution(mesh):
    fine = Mesh(mesh.devices.reshape(SIZES), AXES)
    placed = (P(REP, None, FEAT), P(REP, None, None, FEAT))
    return jax.shard_map(
        per_device, mesh=fine, in_specs=placed, out_specs=P(REP, None, FEAT), check_vma=False
    )
```

```python
import functools

import jax
import jax.numpy as jnp
from jax import lax
from jax.experimental import pallas as pl
from jax.experimental.pallas import tpu as pltpu
from jax.sharding import Mesh, PartitionSpec as P

REP = ("x", "zh")
FEAT = ("zl", "y", "core")
AXES = REP + FEAT
SIZES = (4, 4, 2, 8, 2)
LEARN_RATE = 0.5
HIGHEST = lax.Precision.HIGHEST
SWAP = [(0, 1), (1, 0)]
PLAIN = ((1,), (0,))
ON_ROWS = ((0,), (0,))
ON_COLS = ((1,), (1,))


def dot(left, right, dims, precision=HIGHEST):
    return lax.dot_general(
        left, right, (dims, ((), ())), precision=precision, preferred_element_type=jnp.float32
    )


def split3(value):
    high = value.astype(jnp.bfloat16)
    rest = value - high.astype(jnp.float32)
    middle = rest.astype(jnp.bfloat16)
    low = (rest - middle.astype(jnp.float32)).astype(jnp.bfloat16)
    return high, middle, low


def kernel_call(body, shapes, args, flops, moved):
    return pl.pallas_call(
        body,
        out_shape=shapes,
        in_specs=[pl.BlockSpec(memory_space=pltpu.VMEM)] * len(args),
        out_specs=jax.tree.map(lambda _: pl.BlockSpec(memory_space=pltpu.VMEM), shapes),
        cost_estimate=pl.CostEstimate(flops=flops, bytes_accessed=moved, transcendentals=0),
        compiler_params=pltpu.CompilerParams(vmem_limit_bytes=20 * 1024 * 1024),
    )(*args)


def f32(*shape):
    return jax.ShapeDtypeStruct(shape, jnp.float32)


def products_kernel(start_ref, stream_ref, out_ref):
    rows = jnp.concatenate([stream_ref[0], stream_ref[1]], axis=0)
    right = jnp.concatenate(split3(start_ref[...]) + (stream_ref[0],), axis=0)
    both = dot(rows, right, ON_COLS, None)
    onto = both[:, :64] + (both[:, 64:128] + both[:, 128:192])
    out_ref[:128] = jnp.concatenate([onto[:128], onto[128:]], axis=1)
    out_ref[128:] = both[128:, 192:]


def pack_kernel(received_ref, feat_ref, other_ref, out_ref, sum_ref):
    width = out_ref.shape[2]
    sum_ref[...] = feat_ref[...] + other_ref[...]
    for piece in range(4):
        cols = slice(width * piece, width * piece + width)
        out_ref[piece] = (received_ref[0, :, cols] + received_ref[1, :, cols]) + (
            received_ref[2, :, cols] + received_ref[3, :, cols]
        )


def turn_kernel(received_ref, feat_ref, other_ref, out_ref, sum_ref):
    sum_ref[...] = feat_ref[...] + other_ref[...]
    part = (received_ref[0] + received_ref[1]) + (received_ref[2] + received_ref[3])
    part = part * (1.0 / 16.0)
    for piece in range(4):
        out_ref[piece] = part


def unpack_kernel(received_ref, feat_ref, other_ref, chunk_ref, sum_ref):
    width = received_ref.shape[2]
    sum_ref[...] = feat_ref[...] + other_ref[...]
    for piece in range(4):
        part = received_ref[piece]
        for x in range(4):
            chunk_ref[x, :, width * piece : width * piece + width] = part


def delta_kernel(feat_ref, other_ref, start_ref, stream_ref, out_ref, *, inv_scale, step_size):
    rank = start_ref.shape[0]
    index = lax.broadcasted_iota(jnp.int32, (rank, rank), 0)
    eye = jnp.where(index == lax.broadcasted_iota(jnp.int32, (rank, rank), 1), 1.0, 0.0)
    packed = feat_ref[...] + other_ref[...]
    onto0 = packed[:128, :64]
    onto1 = packed[:128, 64:]
    cross = packed[128:]
    proj0 = onto0 * inv_scale
    cov0 = dot(proj0, proj0, ON_ROWS)
    proj1 = (dot(onto1, eye - step_size * cov0, PLAIN) + step_size * dot(cross, proj0, PLAIN)) * inv_scale
    cov1 = dot(proj1, proj1, ON_ROWS)
    mix_b = step_size * (step_size * dot(cov1, cov0, PLAIN) - cov0 - cov1)
    turned0 = proj0.T
    mix_0 = step_size * (turned0 - step_size * dot(cov1, turned0, PLAIN))
    mix_1 = step_size * proj1.T
    left = jnp.concatenate(split3(jnp.concatenate([mix_0, mix_1], axis=1)), axis=0)
    rows = jnp.concatenate([stream_ref[0], stream_ref[1]], axis=0)
    three = dot(left, rows, PLAIN, None)
    out_ref[...] = dot(mix_b, start_ref[...], PLAIN) + (
        three[:64] + (three[64:128] + three[128:])
    )


def gram_kernel(average_ref, delta_ref, mixed_ref, gram_ref):
    mixed = average_ref[...] + delta_ref[...]
    mixed_ref[...] = mixed
    stacked = jnp.concatenate(split3(mixed), axis=0)
    both = dot(stacked, stacked, ON_COLS, None)
    high_mid = both[:64, 64:128]
    high_low = both[:64, 128:192]
    small = both[64:128, 64:128] + (high_low + both[128:192, :64])
    gram = both[:64, :64] + ((high_mid + both[64:128, :64]) + small)
    lower = jnp.concatenate([gram[:32, :32], gram[32:, :32], gram[32:, 32:]], axis=0)
    gram_ref[...] = jnp.concatenate([lower[24 * part : 24 * part + 24] for part in range(4)], axis=1)


def finish_kernel(parts_ref, mixed_ref, out_ref, *, total_feat):
    packed = parts_ref[0]
    for index in range(1, parts_ref.shape[0]):
        packed = packed + parts_ref[index]
    packed = packed / total_feat
    lower = jnp.concatenate([packed[:, 32 * part : 32 * part + 32] for part in range(4)], axis=0)
    gram = jnp.concatenate(
        [
            jnp.concatenate([lower[:32], lower[32:64].T], axis=1),
            jnp.concatenate([lower[32:64], lower[64:]], axis=1),
        ],
        axis=0,
    )
    lanes = lax.broadcasted_iota(jnp.int32, (8, 128), 1)
    subs = lax.broadcasted_iota(jnp.int32, (8, 128), 0)
    blocks = []
    for b in range(8):
        eye = jnp.where(lanes == subs + (64 + 8 * b), 1.0, 0.0).astype(jnp.float32)
        left = jnp.concatenate([gram[8 * b : 8 * b + 8], jnp.zeros((8, 64), jnp.float32)], axis=1)
        blocks.append(left + eye)
    done = []
    for k in range(64):
        home, sub = divmod(k, 8)
        row = blocks[home][sub : sub + 1, :]
        pivot = row[:, k : k + 1]
        scaled = row / pivot
        for b in range(home, 8):
            col = blocks[b][:, k : k + 1]
            if b == home:
                col = jnp.where(subs[:, :1] > sub, col, 0.0)
            blocks[b] = blocks[b] - col * scaled
        done.append(row[:, 64:] * lax.rsqrt(pivot))
    inverse = jnp.concatenate(done, axis=0)
    out_ref[...] = dot(inverse, mixed_ref[...], PLAIN)


def across(value, distance):
    return lax.ppermute(value, "y", [(y, y ^ distance) for y in range(8)])


def per_device(basis, stream):
    start, batches = basis[0], stream[0]
    rank, width = start.shape
    total_feat = float(width * 32)
    mega = 1 << 20

    arrived = lax.all_to_all(start.reshape(4, 16, width), "x", 0, 0)
    feat = kernel_call(products_kernel, f32(256, 128), (start, batches), 700 * mega, 8 * mega)
    feat = feat + lax.ppermute(feat, "core", SWAP)
    other = lax.ppermute(feat, "zl", SWAP)
    sums = f32(256, 128)
    pieces, feat = kernel_call(
        pack_kernel, (f32(4, 16, width // 4), sums), (arrived, feat, other), mega, mega
    )
    pieces = lax.all_to_all(pieces, "zh", 0, 0)
    pieces, feat = kernel_call(
        turn_kernel, (f32(4, 16, width // 4), sums), (pieces, feat, across(feat, 4)), mega, mega
    )
    pieces = lax.all_to_all(pieces, "zh", 0, 0)
    chunk, feat = kernel_call(
        unpack_kernel, (f32(4, 16, width), sums), (pieces, feat, across(feat, 2)), mega, mega
    )
    average = lax.all_to_all(chunk, "x", 0, 0).reshape(rank, width)
    delta = kernel_call(
        functools.partial(
            delta_kernel, inv_scale=total_feat**-0.5, step_size=LEARN_RATE / batches.shape[1]
        ),
        f32(rank, width),
        (feat, across(feat, 1), start, batches),
        700 * mega,
        8 * mega,
    )
    mixed, gram = kernel_call(
        gram_kernel, (f32(rank, width), f32(24, 128)), (average, delta), 400 * mega, 3 * mega
    )
    gram = gram + lax.ppermute(gram, "core", SWAP)
    parts = lax.all_to_all(jnp.broadcast_to(gram, (16, 24, 128)), ("zl", "y"), 0, 0)
    return kernel_call(
        functools.partial(finish_kernel, total_feat=total_feat),
        f32(rank, width),
        (parts, mixed),
        400 * mega,
        3 * mega,
    )[None]


def solution(mesh):
    fine = Mesh(mesh.devices.reshape(SIZES), AXES)
    placed = (P(REP, None, FEAT), P(REP, None, None, FEAT))
    return jax.shard_map(
        per_device, mesh=fine, in_specs=placed, out_specs=P(REP, None, FEAT), check_vma=False
    )
```

```python
import functools

import jax
import jax.numpy as jnp
from jax import lax
from jax.experimental import pallas as pl
from jax.experimental.pallas import tpu as pltpu
from jax.sharding import Mesh, PartitionSpec as P

REP = ("x", "zh")
FEAT = ("zl", "y", "core")
AXES = REP + FEAT
SIZES = (4, 4, 2, 8, 2)
LEARN_RATE = 0.5
HIGHEST = lax.Precision.HIGHEST
SWAP = [(0, 1), (1, 0)]
PAIRS = (
    [(1, 6), (2, 5), (0, 3), (4, 7)],
    [(1, 2), (3, 4), (5, 6), (7, 0)],
    [(0, 1), (2, 3), (4, 5), (6, 7)],
)
PLAIN = ((1,), (0,))
ON_ROWS = ((0,), (0,))
ON_COLS = ((1,), (1,))


def dot(left, right, dims, precision=HIGHEST):
    return lax.dot_general(
        left, right, (dims, ((), ())), precision=precision, preferred_element_type=jnp.float32
    )


def split3(value):
    high = value.astype(jnp.bfloat16)
    rest = value - high.astype(jnp.float32)
    middle = rest.astype(jnp.bfloat16)
    low = (rest - middle.astype(jnp.float32)).astype(jnp.bfloat16)
    return high, middle, low


def exact_dot(left, right):
    high, middle, low = split3(left)
    left = jnp.concatenate([high, high, high, middle, middle, low], axis=1)
    high, middle, low = split3(right)
    right = jnp.concatenate([high, middle, low, high, middle, high], axis=0)
    return dot(left, right, PLAIN, None)


IN_HBM = pl.BlockSpec(memory_space=pltpu.HBM)
IN_VMEM = pl.BlockSpec(memory_space=pltpu.VMEM)
CHUNKS = 4
LARGE = 55000 << 10
DELTA_LIMIT = 54500 << 10
GRAM_LIMIT = 53000 << 10
FINISH_LIMIT = 53000 << 10


def kernel_call(body, ins, outs, args, flops, moved, scratch=(), limit=20 << 20):
    return pl.pallas_call(
        body,
        out_shape=tuple(f32(*shape) for shape, _ in outs),
        in_specs=list(ins),
        out_specs=tuple(space for _, space in outs),
        scratch_shapes=list(scratch),
        cost_estimate=pl.CostEstimate(flops=flops, bytes_accessed=moved, transcendentals=0),
        compiler_params=pltpu.CompilerParams(vmem_limit_bytes=limit),
    )(*args)


def fetch(pairs, sems):
    copies = [
        pltpu.make_async_copy(source, target, sems.at[index])
        for index, (source, target) in enumerate(pairs)
    ]
    for copy in copies:
        copy.start()
    return copies


def f32(*shape):
    return jax.ShapeDtypeStruct(shape, jnp.float32)


def products_kernel(start_ref, stream_ref, out_ref, start_vmem, stream_vmem, sems):
    width = start_vmem.shape[1] // CHUNKS
    spans = [slice(width * c, width * c + width) for c in range(CHUNKS)]
    copies = fetch(
        [(start_ref.at[:, s], start_vmem.at[:, s]) for s in spans]
        + [(stream_ref.at[:, :, s], stream_vmem.at[:, :, s]) for s in spans],
        sems,
    )
    both = None
    for c, span in enumerate(spans):
        copies[c].wait()
        copies[CHUNKS + c].wait()
        first = stream_vmem[0, :, span]
        rows = jnp.concatenate([first, stream_vmem[1, :, span]], axis=0)
        right = jnp.concatenate(split3(start_vmem[:, span]) + (first,), axis=0)
        part = dot(rows, right, ON_COLS, None)
        both = part if both is None else both + part
    onto = both[:, :64] + (both[:, 64:128] + both[:, 128:192])
    out_ref[:128] = jnp.concatenate([onto[:128], onto[128:]], axis=1)
    out_ref[128:] = both[128:, 192:]


def pack_kernel(received_ref, feat_ref, other_ref, out_ref, sum_ref, total, sems):
    sum_ref[...] = feat_ref[...] + other_ref[...]
    width = total.shape[2]
    copies = []
    for piece in range(4):
        cols = slice(width * piece, width * piece + width)
        total[piece] = (received_ref[0, :, cols] + received_ref[1, :, cols]) + (
            received_ref[2, :, cols] + received_ref[3, :, cols]
        )
        copy = pltpu.make_async_copy(total.at[piece], out_ref.at[piece], sems.at[piece])
        copy.start()
        copies.append(copy)
    for copy in copies:
        copy.wait()


def turn_kernel(received_ref, feat_ref, other_ref, out_ref, sum_ref, total, sems):
    sum_ref[...] = feat_ref[...] + other_ref[...]
    part = (received_ref[0] + received_ref[1]) + (received_ref[2] + received_ref[3])
    total[...] = part * (1.0 / 16.0)
    for copy in fetch([(total, out_ref.at[piece]) for piece in range(4)], sems):
        copy.wait()


def unpack_kernel(received_ref, feat_ref, other_ref, out_ref, sum_ref, sems):
    width = received_ref.shape[2]
    pairs = []
    for piece in range(4):
        for x in range(4):
            pairs.append(
                (received_ref.at[piece], out_ref.at[x, :, width * piece : width * piece + width])
            )
    copies = fetch(pairs, sems)
    sum_ref[...] = feat_ref[...] + other_ref[...]
    for copy in copies:
        copy.wait()


def delta_kernel(
    feat_ref, other_ref, start_ref, stream_ref, out_ref, start_vmem, stream_vmem, delta, sems, out_sems,
    *, inv_scale, step_size
):
    width = delta.shape[1] // CHUNKS
    spans = [slice(width * c, width * c + width) for c in range(CHUNKS)]
    pairs = []
    for span in spans:
        pairs.append((start_ref.at[:, span], start_vmem.at[:, span]))
        pairs.append((stream_ref.at[:, :, span], stream_vmem.at[:, :, span]))
    arriving = fetch(pairs, sems)
    rank = start_ref.shape[0]
    index = lax.broadcasted_iota(jnp.int32, (rank, rank), 0)
    eye = jnp.where(index == lax.broadcasted_iota(jnp.int32, (rank, rank), 1), 1.0, 0.0)
    onto0 = feat_ref[:128, :64] + other_ref[:128, :64]
    onto1 = feat_ref[:128, 64:] + other_ref[:128, 64:]
    cross = feat_ref[128:] + other_ref[128:]
    proj0 = onto0 * inv_scale
    cov0 = dot(proj0, proj0, ON_ROWS)
    proj1 = (dot(onto1, eye - step_size * cov0, PLAIN) + step_size * dot(cross, proj0, PLAIN)) * inv_scale
    cov1 = dot(proj1, proj1, ON_ROWS)
    mix_b = step_size * (step_size * dot(cov1, cov0, PLAIN) - cov0 - cov1)
    turned0 = proj0.T
    mix_0 = step_size * (turned0 - step_size * dot(cov1, turned0, PLAIN))
    mix_1 = step_size * proj1.T
    left = jnp.concatenate(split3(jnp.concatenate([mix_0, mix_1], axis=1)), axis=0)
    copies = []
    for c, span in enumerate(spans):
        arriving[2 * c].wait()
        arriving[2 * c + 1].wait()
        rows = jnp.concatenate([stream_vmem[0, :, span], stream_vmem[1, :, span]], axis=0)
        three = dot(left, rows, PLAIN, None)
        delta[:, span] = exact_dot(mix_b, start_vmem[:, span]) + (
            three[:64] + (three[64:128] + three[128:])
        )
        copy = pltpu.make_async_copy(delta.at[:, span], out_ref.at[:, span], out_sems.at[c])
        copy.start()
        copies.append(copy)
    for copy in copies:
        copy.wait()


def gram_kernel(average_ref, delta_ref, mixed_ref, gram_ref, delta, sems):
    width = delta.shape[1] // CHUNKS
    spans = [slice(width * c, width * c + width) for c in range(CHUNKS)]
    copies = fetch([(delta_ref.at[:, s], delta.at[:, s]) for s in spans], sems)
    both = None
    for copy, span in zip(copies, spans):
        copy.wait()
        mixed = average_ref[:, span] + delta[:, span]
        mixed_ref[:, span] = mixed
        stacked = jnp.concatenate(split3(mixed), axis=0)
        part = dot(stacked, stacked, ON_COLS, None)
        both = part if both is None else both + part
    high_mid = both[:64, 64:128]
    high_low = both[:64, 128:192]
    small = both[64:128, 64:128] + (high_low + both[128:192, :64])
    gram = both[:64, :64] + ((high_mid + both[64:128, :64]) + small)
    lower = jnp.concatenate([gram[:32, :32], gram[32:, :32], gram[32:, 32:]], axis=0)
    packed = jnp.concatenate([lower[24 * part : 24 * part + 24] for part in range(4)], axis=1)
    for copy in range(4):
        gram_ref[copy] = packed


def inverse_factor(gram):
    lanes = lax.broadcasted_iota(jnp.int32, (8, 128), 1)
    subs = lax.broadcasted_iota(jnp.int32, (8, 128), 0)
    blocks = []
    for b in range(8):
        eye = jnp.where(lanes == subs + (64 + 8 * b), 1.0, 0.0).astype(jnp.float32)
        left = jnp.concatenate([gram[8 * b : 8 * b + 8], jnp.zeros((8, 64), jnp.float32)], axis=1)
        blocks.append(left + eye)
    done = []
    for panel in range(8):
        cols = []
        for j in range(8):
            k = 8 * panel + j
            cols.append([jnp.broadcast_to(block[:, k : k + 1], (8, 128)) for block in blocks[panel:]])
        for j in range(8):
            row = jnp.broadcast_to(blocks[panel][j : j + 1, :], (8, 128))
            pivot = jnp.broadcast_to(cols[j][0][j : j + 1, :], (8, 128))
            done.append((row * lax.rsqrt(pivot))[:1, 64:])
            inverse = 1.0 / pivot
            factors = [col * inverse for col in cols[j]]
            factors[0] = jnp.where(subs > j, factors[0], 0.0)
            for later in range(j + 1, 8):
                entry = jnp.broadcast_to(cols[later][0][j : j + 1, :], (8, 128))
                cols[later] = [col - f * entry for col, f in zip(cols[later], factors)]
            for i, f in enumerate(factors):
                blocks[panel + i] = blocks[panel + i] - f * row
    return jnp.concatenate(done, axis=0)


def finish_kernel(parts_ref, mixed_ref, out_ref, result, sems, *, total_feat):
    packed = parts_ref[0]
    for index in range(1, parts_ref.shape[0]):
        packed = packed + parts_ref[index]
    packed = packed / total_feat
    lower = jnp.concatenate([packed[:, 32 * part : 32 * part + 32] for part in range(4)], axis=0)
    gram = jnp.concatenate(
        [
            jnp.concatenate([lower[:32], lower[32:64].T], axis=1),
            jnp.concatenate([lower[32:64], lower[64:]], axis=1),
        ],
        axis=0,
    )
    inverse = inverse_factor(gram)
    width = result.shape[1] // CHUNKS
    copies = []
    for c in range(CHUNKS):
        span = slice(width * c, width * c + width)
        result[:, span] = exact_dot(inverse, mixed_ref[:, span])
        copy = pltpu.make_async_copy(result.at[:, span], out_ref.at[:, span], sems.at[c])
        copy.start()
        copies.append(copy)
    for copy in copies:
        copy.wait()


def fold_kernel(parts_ref, out_ref):
    total = (parts_ref[0] + parts_ref[1]) + (parts_ref[2] + parts_ref[3])
    for index in range(8):
        out_ref[index] = total


def across(value, pairs):
    return lax.ppermute(value, "y", pairs + [(b, a) for a, b in pairs])


def per_device(basis, stream):
    start, batches = basis[0], stream[0]
    rank, width = start.shape
    total_feat = float(width * 32)
    mega = 1 << 20
    dma = pltpu.SemaphoreType.DMA
    held_start = pltpu.VMEM(start.shape, jnp.float32)
    held_stream = pltpu.VMEM(batches.shape, jnp.bfloat16)
    quarter = (4, 16, width // 4)

    arrived = lax.all_to_all(start.reshape(4, 16, width), "x", 0, 0)
    (feat,) = kernel_call(
        products_kernel,
        (IN_HBM, IN_HBM),
        [((256, 128), IN_VMEM)],
        (start, batches),
        700 * mega,
        8 * mega,
        (held_start, held_stream, dma((2 * CHUNKS,))),
        LARGE,
    )
    feat = feat + lax.ppermute(feat, "core", SWAP)
    pieces, feat = kernel_call(
        pack_kernel,
        (IN_VMEM,) * 3,
        [(quarter, IN_HBM), ((256, 128), IN_VMEM)],
        (arrived, feat, lax.ppermute(feat, "zl", SWAP)),
        mega,
        2 * mega,
        (pltpu.VMEM(quarter, jnp.float32), dma((4,))),
    )
    pieces = lax.all_to_all(pieces, "zh", 0, 0)
    pieces, feat = kernel_call(
        turn_kernel,
        (IN_VMEM,) * 3,
        [(quarter, IN_HBM), ((256, 128), IN_VMEM)],
        (pieces, feat, across(feat, PAIRS[0])),
        mega,
        2 * mega,
        (pltpu.VMEM(quarter[1:], jnp.float32), dma((4,))),
    )
    pieces = lax.all_to_all(pieces, "zh", 0, 0)
    chunk, feat = kernel_call(
        unpack_kernel,
        (IN_VMEM,) * 3,
        [((4, 16, width), IN_HBM), ((256, 128), IN_VMEM)],
        (pieces, feat, across(feat, PAIRS[1])),
        mega,
        2 * mega,
        (dma((16,)),),
        53500 << 10,
    )
    average = lax.all_to_all(chunk, "x", 0, 0).reshape(rank, width)
    (delta,) = kernel_call(
        functools.partial(
            delta_kernel, inv_scale=total_feat**-0.5, step_size=LEARN_RATE / batches.shape[1]
        ),
        (IN_VMEM, IN_VMEM, IN_HBM, IN_HBM),
        [((rank, width), IN_HBM)],
        (feat, across(feat, PAIRS[2]), start, batches),
        700 * mega,
        8 * mega,
        (held_start, held_stream, held_start, dma((2 * CHUNKS,)), dma((CHUNKS,))),
        DELTA_LIMIT,
    )
    mixed, gram = kernel_call(
        gram_kernel,
        (IN_VMEM, IN_HBM),
        [((rank, width), IN_VMEM), ((4, 24, 128), IN_VMEM)],
        (average, delta),
        400 * mega,
        3 * mega,
        (held_start, dma((CHUNKS,))),
        GRAM_LIMIT,
    )
    gram = lax.all_to_all(gram, ("zl", "core"), 0, 0)
    (gram,) = kernel_call(fold_kernel, (IN_VMEM,), [((8, 24, 128), IN_VMEM)], (gram,), mega, mega)
    parts = lax.all_to_all(gram, "y", 0, 0)
    (result,) = kernel_call(
        functools.partial(finish_kernel, total_feat=total_feat),
        (IN_VMEM, IN_VMEM),
        [((rank, width), IN_HBM)],
        (parts, mixed),
        400 * mega,
        3 * mega,
        (held_start, dma((CHUNKS,))),
        FINISH_LIMIT,
    )
    return result[None]


def solution(mesh):
    fine = Mesh(mesh.devices.reshape(SIZES), AXES)
    placed = (P(REP, None, FEAT), P(REP, None, None, FEAT))
    return jax.shard_map(
        per_device, mesh=fine, in_specs=placed, out_specs=P(REP, None, FEAT), check_vma=False
    )
```

```python
import functools

import jax
import jax.numpy as jnp
from jax import lax
from jax.experimental import pallas as pl
from jax.experimental.pallas import tpu as pltpu
from jax.sharding import Mesh, PartitionSpec as P

REP = ("x", "zh")
FEAT = ("zl", "y", "core")
AXES = REP + FEAT
SIZES = (4, 4, 2, 8, 2)
LEARN_RATE = 0.5
HIGHEST = lax.Precision.HIGHEST
SWAP = [(0, 1), (1, 0)]
PAIRS = (
    [(1, 6), (2, 5), (0, 3), (4, 7)],
    [(1, 2), (3, 4), (5, 6), (7, 0)],
    [(0, 1), (2, 3), (4, 5), (6, 7)],
)
PLAIN = ((1,), (0,))
ON_ROWS = ((0,), (0,))
ON_COLS = ((1,), (1,))


def dot(left, right, dims, precision=HIGHEST):
    return lax.dot_general(
        left, right, (dims, ((), ())), precision=precision, preferred_element_type=jnp.float32
    )


def split3(value):
    high = value.astype(jnp.bfloat16)
    rest = value - high.astype(jnp.float32)
    middle = rest.astype(jnp.bfloat16)
    low = (rest - middle.astype(jnp.float32)).astype(jnp.bfloat16)
    return high, middle, low


def exact_dot(left, right):
    high, middle, low = split3(left)
    left = jnp.concatenate([high, high, high, middle, middle, low], axis=1)
    high, middle, low = split3(right)
    right = jnp.concatenate([high, middle, low, high, middle, high], axis=0)
    return dot(left, right, PLAIN, None)


IN_HBM = pl.BlockSpec(memory_space=pltpu.HBM)
IN_VMEM = pl.BlockSpec(memory_space=pltpu.VMEM)
CHUNKS = 4
LARGE = 55000 << 10
FIRST_LIMIT = 53000 << 10
DELTA_LIMIT = 53000 << 10
GRAM_LIMIT = 50000 << 10
FINISH_LIMIT = 53000 << 10


def kernel_call(body, ins, outs, args, flops, moved, scratch=(), limit=20 << 20):
    return pl.pallas_call(
        body,
        out_shape=tuple(f32(*shape) for shape, _ in outs),
        in_specs=list(ins),
        out_specs=tuple(space for _, space in outs),
        scratch_shapes=list(scratch),
        cost_estimate=pl.CostEstimate(flops=flops, bytes_accessed=moved, transcendentals=0),
        compiler_params=pltpu.CompilerParams(vmem_limit_bytes=limit),
    )(*args)


def fetch(pairs, sems):
    copies = [
        pltpu.make_async_copy(source, target, sems.at[index])
        for index, (source, target) in enumerate(pairs)
    ]
    for copy in copies:
        copy.start()
    return copies


def f32(*shape):
    return jax.ShapeDtypeStruct(shape, jnp.float32)


def products_kernel(start_ref, stream_ref, out_ref, stream_vmem, sems):
    width = start_ref.shape[1] // CHUNKS
    spans = [slice(width * c, width * c + width) for c in range(CHUNKS)]
    copies = fetch([(stream_ref.at[:, :, s], stream_vmem.at[:, :, s]) for s in spans], sems)
    both = None
    for c, span in enumerate(spans):
        copies[c].wait()
        first = stream_vmem[0, :, span]
        rows = jnp.concatenate([first, stream_vmem[1, :, span]], axis=0)
        right = jnp.concatenate(split3(start_ref[:, span]) + (first,), axis=0)
        part = dot(rows, right, ON_COLS, None)
        both = part if both is None else both + part
    onto = both[:, :64] + (both[:, 64:128] + both[:, 128:192])
    out_ref[:128] = jnp.concatenate([onto[:128], onto[128:]], axis=1)
    out_ref[128:] = both[128:, 192:]


def pack_kernel(received_ref, feat_ref, other_ref, out_ref, sum_ref, total, sems):
    sum_ref[...] = feat_ref[...] + other_ref[...]
    width = total.shape[2]
    copies = []
    for piece in range(4):
        cols = slice(width * piece, width * piece + width)
        total[piece] = (received_ref[0, :, cols] + received_ref[1, :, cols]) + (
            received_ref[2, :, cols] + received_ref[3, :, cols]
        )
        copy = pltpu.make_async_copy(total.at[piece], out_ref.at[piece], sems.at[piece])
        copy.start()
        copies.append(copy)
    for copy in copies:
        copy.wait()


def turn_kernel(received_ref, feat_ref, other_ref, out_ref, sum_ref, total, sems):
    sum_ref[...] = feat_ref[...] + other_ref[...]
    part = (received_ref[0] + received_ref[1]) + (received_ref[2] + received_ref[3])
    total[...] = part * (1.0 / 16.0)
    for copy in fetch([(total, out_ref.at[piece]) for piece in range(4)], sems):
        copy.wait()


def unpack_kernel(received_ref, feat_ref, other_ref, out_ref, sum_ref, sems):
    width = received_ref.shape[2]
    pairs = []
    for piece in range(4):
        for x in range(4):
            pairs.append(
                (received_ref.at[piece], out_ref.at[x, :, width * piece : width * piece + width])
            )
    copies = fetch(pairs, sems)
    sum_ref[...] = feat_ref[...] + other_ref[...]
    for copy in copies:
        copy.wait()


def delta_kernel(
    feat_ref, other_ref, start_ref, stream_ref, out_ref, start_vmem, stream_vmem, sems,
    *, inv_scale, step_size
):
    width = out_ref.shape[1] // CHUNKS
    spans = [slice(width * c, width * c + width) for c in range(CHUNKS)]
    pairs = []
    for span in spans:
        pairs.append((start_ref.at[:, span], start_vmem.at[:, span]))
        pairs.append((stream_ref.at[:, :, span], stream_vmem.at[:, :, span]))
    arriving = fetch(pairs, sems)
    rank = start_ref.shape[0]
    index = lax.broadcasted_iota(jnp.int32, (rank, rank), 0)
    eye = jnp.where(index == lax.broadcasted_iota(jnp.int32, (rank, rank), 1), 1.0, 0.0)
    onto0 = feat_ref[:128, :64] + other_ref[:128, :64]
    onto1 = feat_ref[:128, 64:] + other_ref[:128, 64:]
    cross = feat_ref[128:] + other_ref[128:]
    proj0 = onto0 * inv_scale
    cov0 = dot(proj0, proj0, ON_ROWS)
    proj1 = (dot(onto1, eye - step_size * cov0, PLAIN) + step_size * dot(cross, proj0, PLAIN)) * inv_scale
    cov1 = dot(proj1, proj1, ON_ROWS)
    mix_b = step_size * (step_size * dot(cov1, cov0, PLAIN) - cov0 - cov1)
    turned0 = proj0.T
    mix_0 = step_size * (turned0 - step_size * dot(cov1, turned0, PLAIN))
    mix_1 = step_size * proj1.T
    left = jnp.concatenate(split3(jnp.concatenate([mix_0, mix_1], axis=1)), axis=0)
    for c, span in enumerate(spans):
        arriving[2 * c].wait()
        arriving[2 * c + 1].wait()
        rows = jnp.concatenate([stream_vmem[0, :, span], stream_vmem[1, :, span]], axis=0)
        three = dot(left, rows, PLAIN, None)
        out_ref[:, span] = exact_dot(mix_b, start_vmem[:, span]) + (
            three[:64] + (three[64:128] + three[128:])
        )


def gram_kernel(average_ref, delta_ref, mixed_ref, gram_ref):
    mixed = average_ref[...] + delta_ref[...]
    mixed_ref[...] = mixed
    stacked = jnp.concatenate(split3(mixed), axis=0)
    both = dot(stacked, stacked, ON_COLS, None)
    high_mid = both[:64, 64:128]
    high_low = both[:64, 128:192]
    small = both[64:128, 64:128] + (high_low + both[128:192, :64])
    gram = both[:64, :64] + ((high_mid + both[64:128, :64]) + small)
    lower = jnp.concatenate([gram[:32, :32], gram[32:, :32], gram[32:, 32:]], axis=0)
    packed = jnp.concatenate([lower[24 * part : 24 * part + 24] for part in range(4)], axis=1)
    for copy in range(4):
        gram_ref[copy] = packed


def inverse_factor(gram):
    lanes = lax.broadcasted_iota(jnp.int32, (8, 128), 1)
    subs = lax.broadcasted_iota(jnp.int32, (8, 128), 0)
    blocks = []
    for b in range(8):
        eye = jnp.where(lanes == subs + (64 + 8 * b), 1.0, 0.0).astype(jnp.float32)
        left = jnp.concatenate([gram[8 * b : 8 * b + 8], jnp.zeros((8, 64), jnp.float32)], axis=1)
        blocks.append(left + eye)
    done = []
    for panel in range(8):
        cols = []
        for j in range(8):
            k = 8 * panel + j
            cols.append([jnp.broadcast_to(block[:, k : k + 1], (8, 128)) for block in blocks[panel:]])
        for j in range(8):
            row = jnp.broadcast_to(blocks[panel][j : j + 1, :], (8, 128))
            pivot = jnp.broadcast_to(cols[j][0][j : j + 1, :], (8, 128))
            done.append((row * lax.rsqrt(pivot))[:1, 64:])
            inverse = 1.0 / pivot
            factors = [col * inverse for col in cols[j]]
            factors[0] = jnp.where(subs > j, factors[0], 0.0)
            for later in range(j + 1, 8):
                entry = jnp.broadcast_to(cols[later][0][j : j + 1, :], (8, 128))
                cols[later] = [col - f * entry for col, f in zip(cols[later], factors)]
            for i, f in enumerate(factors):
                blocks[panel + i] = blocks[panel + i] - f * row
    return jnp.concatenate(done, axis=0)


def finish_kernel(parts_ref, mixed_ref, out_ref, result, sems, *, total_feat):
    packed = parts_ref[0]
    for index in range(1, parts_ref.shape[0]):
        packed = packed + parts_ref[index]
    packed = packed / total_feat
    lower = jnp.concatenate([packed[:, 32 * part : 32 * part + 32] for part in range(4)], axis=0)
    gram = jnp.concatenate(
        [
            jnp.concatenate([lower[:32], lower[32:64].T], axis=1),
            jnp.concatenate([lower[32:64], lower[64:]], axis=1),
        ],
        axis=0,
    )
    inverse = inverse_factor(gram)
    width = result.shape[1] // CHUNKS
    copies = []
    for c in range(CHUNKS):
        span = slice(width * c, width * c + width)
        result[:, span] = exact_dot(inverse, mixed_ref[:, span])
        copy = pltpu.make_async_copy(result.at[:, span], out_ref.at[:, span], sems.at[c])
        copy.start()
        copies.append(copy)
    for copy in copies:
        copy.wait()


def fold_kernel(parts_ref, out_ref):
    total = (parts_ref[0] + parts_ref[1]) + (parts_ref[2] + parts_ref[3])
    for index in range(8):
        out_ref[index] = total


def across(value, pairs):
    return lax.ppermute(value, "y", pairs + [(b, a) for a, b in pairs])


def per_device(basis, stream):
    start, batches = basis[0], stream[0]
    rank, width = start.shape
    total_feat = float(width * 32)
    mega = 1 << 20
    dma = pltpu.SemaphoreType.DMA
    held_start = pltpu.VMEM(start.shape, jnp.float32)
    held_stream = pltpu.VMEM(batches.shape, jnp.bfloat16)
    quarter = (4, 16, width // 4)

    arrived = lax.all_to_all(start.reshape(4, 16, width), "x", 0, 0)
    (feat,) = kernel_call(
        products_kernel,
        (IN_VMEM, IN_HBM),
        [((256, 128), IN_VMEM)],
        (start, batches),
        700 * mega,
        8 * mega,
        (held_stream, dma((CHUNKS,))),
        FIRST_LIMIT,
    )
    feat = feat + lax.ppermute(feat, "core", SWAP)
    pieces, feat = kernel_call(
        pack_kernel,
        (IN_VMEM,) * 3,
        [(quarter, IN_HBM), ((256, 128), IN_VMEM)],
        (arrived, feat, lax.ppermute(feat, "zl", SWAP)),
        mega,
        2 * mega,
        (pltpu.VMEM(quarter, jnp.float32), dma((4,))),
    )
    pieces = lax.all_to_all(pieces, "zh", 0, 0)
    pieces, feat = kernel_call(
        turn_kernel,
        (IN_VMEM,) * 3,
        [(quarter, IN_HBM), ((256, 128), IN_VMEM)],
        (pieces, feat, across(feat, PAIRS[0])),
        mega,
        2 * mega,
        (pltpu.VMEM(quarter[1:], jnp.float32), dma((4,))),
    )
    pieces = lax.all_to_all(pieces, "zh", 0, 0)
    chunk, feat = kernel_call(
        unpack_kernel,
        (IN_VMEM,) * 3,
        [((4, 16, width), IN_HBM), ((256, 128), IN_VMEM)],
        (pieces, feat, across(feat, PAIRS[1])),
        mega,
        2 * mega,
        (dma((16,)),),
        53500 << 10,
    )
    average = lax.all_to_all(chunk, "x", 0, 0).reshape(rank, width)
    (delta,) = kernel_call(
        functools.partial(
            delta_kernel, inv_scale=total_feat**-0.5, step_size=LEARN_RATE / batches.shape[1]
        ),
        (IN_VMEM, IN_VMEM, IN_HBM, IN_HBM),
        [((rank, width), IN_VMEM)],
        (feat, across(feat, PAIRS[2]), start, batches),
        700 * mega,
        8 * mega,
        (held_start, held_stream, dma((2 * CHUNKS,))),
        DELTA_LIMIT,
    )
    mixed, gram = kernel_call(
        gram_kernel,
        (IN_VMEM, IN_VMEM),
        [((rank, width), IN_VMEM), ((4, 24, 128), IN_VMEM)],
        (average, delta),
        400 * mega,
        3 * mega,
        (),
        GRAM_LIMIT,
    )
    gram = lax.all_to_all(gram, ("zl", "core"), 0, 0)
    (gram,) = kernel_call(fold_kernel, (IN_VMEM,), [((8, 24, 128), IN_VMEM)], (gram,), mega, mega)
    parts = lax.all_to_all(gram, "y", 0, 0)
    (result,) = kernel_call(
        functools.partial(finish_kernel, total_feat=total_feat),
        (IN_VMEM, IN_VMEM),
        [((rank, width), IN_HBM)],
        (parts, mixed),
        400 * mega,
        3 * mega,
        (held_start, dma((CHUNKS,))),
        FINISH_LIMIT,
    )
    return result[None]


def solution(mesh):
    fine = Mesh(mesh.devices.reshape(SIZES), AXES)
    placed = (P(REP, None, FEAT), P(REP, None, None, FEAT))
    return jax.shard_map(
        per_device, mesh=fine, in_specs=placed, out_specs=P(REP, None, FEAT), check_vma=False
    )
```

```python
import functools

import jax
import jax.numpy as jnp
from jax import lax
from jax.experimental import pallas as pl
from jax.experimental.pallas import tpu as pltpu
from jax.sharding import Mesh, PartitionSpec as P

REP = ("x", "zh")
FEAT = ("zl", "y", "core")
AXES = REP + FEAT
SIZES = (4, 4, 2, 8, 2)
LEARN_RATE = 0.5
HIGHEST = lax.Precision.HIGHEST
SWAP = [(0, 1), (1, 0)]
PAIRS = (
    [(0, 1), (2, 3), (4, 5), (6, 7)],
    [(1, 2), (3, 4), (5, 6), (7, 0)],
    [(1, 6), (2, 5), (0, 3), (4, 7)],
)
PLAIN = ((1,), (0,))
ON_ROWS = ((0,), (0,))
ON_COLS = ((1,), (1,))


def dot(left, right, dims, precision=HIGHEST):
    return lax.dot_general(
        left, right, (dims, ((), ())), precision=precision, preferred_element_type=jnp.float32
    )


def split3(value):
    high = value.astype(jnp.bfloat16)
    rest = value - high.astype(jnp.float32)
    middle = rest.astype(jnp.bfloat16)
    low = (rest - middle.astype(jnp.float32)).astype(jnp.bfloat16)
    return high, middle, low


def exact_dot(left, right):
    high, middle, low = split3(left)
    left = jnp.concatenate([high, high, high, middle, middle, low], axis=1)
    high, middle, low = split3(right)
    right = jnp.concatenate([high, middle, low, high, middle, high], axis=0)
    return dot(left, right, PLAIN, None)


IN_HBM = pl.BlockSpec(memory_space=pltpu.HBM)
IN_VMEM = pl.BlockSpec(memory_space=pltpu.VMEM)
CHUNKS = 4
LARGE = 55000 << 10
FIRST_LIMIT = 53000 << 10
DELTA_LIMIT = 52000 << 10
GRAM_LIMIT = 50000 << 10
FINISH_LIMIT = 53000 << 10


def kernel_call(body, ins, outs, args, flops, moved, scratch=(), limit=20 << 20):
    return pl.pallas_call(
        body,
        out_shape=tuple(f32(*shape) for shape, _ in outs),
        in_specs=list(ins),
        out_specs=tuple(space for _, space in outs),
        scratch_shapes=list(scratch),
        cost_estimate=pl.CostEstimate(flops=flops, bytes_accessed=moved, transcendentals=0),
        compiler_params=pltpu.CompilerParams(vmem_limit_bytes=limit),
    )(*args)


def fetch(pairs, sems):
    copies = [
        pltpu.make_async_copy(source, target, sems.at[index])
        for index, (source, target) in enumerate(pairs)
    ]
    for copy in copies:
        copy.start()
    return copies


def f32(*shape):
    return jax.ShapeDtypeStruct(shape, jnp.float32)


def products_kernel(start_ref, stream_ref, out_ref, stream_vmem, sems):
    width = start_ref.shape[1] // CHUNKS
    spans = [slice(width * c, width * c + width) for c in range(CHUNKS)]
    copies = fetch([(stream_ref.at[:, :, s], stream_vmem.at[:, :, s]) for s in spans], sems)
    both = None
    for c, span in enumerate(spans):
        copies[c].wait()
        first = stream_vmem[0, :, span]
        rows = jnp.concatenate([first, stream_vmem[1, :, span]], axis=0)
        right = jnp.concatenate(split3(start_ref[:, span]) + (first,), axis=0)
        part = dot(rows, right, ON_COLS, None)
        both = part if both is None else both + part
    onto = both[:, :64] + (both[:, 64:128] + both[:, 128:192])
    out_ref[:128] = jnp.concatenate([onto[:128], onto[128:]], axis=1)
    out_ref[128:] = both[128:, 192:]


def pack_kernel(received_ref, feat_ref, other_ref, out_ref, sum_ref, total, sems):
    sum_ref[...] = feat_ref[...] + other_ref[...]
    width = total.shape[2]
    copies = []
    for piece in range(4):
        cols = slice(width * piece, width * piece + width)
        total[piece] = (received_ref[0, :, cols] + received_ref[1, :, cols]) + (
            received_ref[2, :, cols] + received_ref[3, :, cols]
        )
        copy = pltpu.make_async_copy(total.at[piece], out_ref.at[piece], sems.at[piece])
        copy.start()
        copies.append(copy)
    for copy in copies:
        copy.wait()


def turn_kernel(received_ref, feat_ref, other_ref, out_ref, sum_ref, total, sems):
    sum_ref[...] = feat_ref[...] + other_ref[...]
    part = (received_ref[0] + received_ref[1]) + (received_ref[2] + received_ref[3])
    total[...] = part * (1.0 / 16.0)
    for copy in fetch([(total, out_ref.at[piece]) for piece in range(4)], sems):
        copy.wait()


def unpack_kernel(received_ref, feat_ref, other_ref, out_ref, sum_ref, sems):
    copies = fetch([(received_ref, out_ref.at[x]) for x in range(4)], sems)
    sum_ref[...] = feat_ref[...] + other_ref[...]
    for copy in copies:
        copy.wait()


def delta_kernel(
    feat_ref, other_ref, start_ref, stream_ref, out_ref, stream_vmem, sems,
    *, inv_scale, step_size
):
    width = out_ref.shape[1] // CHUNKS
    spans = [slice(width * c, width * c + width) for c in range(CHUNKS)]
    arriving = fetch([(stream_ref.at[:, :, s], stream_vmem.at[:, :, s]) for s in spans], sems)
    rank = start_ref.shape[0]
    index = lax.broadcasted_iota(jnp.int32, (rank, rank), 0)
    eye = jnp.where(index == lax.broadcasted_iota(jnp.int32, (rank, rank), 1), 1.0, 0.0)
    onto0 = feat_ref[:128, :64] + other_ref[:128, :64]
    onto1 = feat_ref[:128, 64:] + other_ref[:128, 64:]
    cross = feat_ref[128:] + other_ref[128:]
    proj0 = onto0 * inv_scale
    cov0 = dot(proj0, proj0, ON_ROWS)
    proj1 = (dot(onto1, eye - step_size * cov0, PLAIN) + step_size * dot(cross, proj0, PLAIN)) * inv_scale
    cov1 = dot(proj1, proj1, ON_ROWS)
    mix_b = step_size * (step_size * dot(cov1, cov0, PLAIN) - cov0 - cov1)
    turned0 = proj0.T
    mix_0 = step_size * (turned0 - step_size * dot(cov1, turned0, PLAIN))
    mix_1 = step_size * proj1.T
    left = jnp.concatenate([mix_b, mix_b, mix_b, mix_0, mix_1], axis=1)
    left = jnp.concatenate(split3(left), axis=0)
    for c, span in enumerate(spans):
        arriving[c].wait()
        right = split3(start_ref[:, span]) + (stream_vmem[0, :, span], stream_vmem[1, :, span])
        three = dot(left, jnp.concatenate(right, axis=0), PLAIN, None)
        out_ref[:, span] = three[:64] + (three[64:128] + three[128:])


def gram_kernel(average_ref, delta_ref, mixed_ref, gram_ref):
    parts, pieces, rows, width = average_ref.shape
    for part in range(parts):
        for piece in range(pieces):
            place = (slice(rows * part, rows * part + rows), slice(width * piece, width * piece + width))
            mixed_ref[place] = average_ref[part, piece] + delta_ref[place]
    stacked = jnp.concatenate(split3(mixed_ref[...]), axis=0)
    both = dot(stacked, stacked, ON_COLS, None)
    high_mid = both[:64, 64:128]
    high_low = both[:64, 128:192]
    small = both[64:128, 64:128] + (high_low + both[128:192, :64])
    gram = both[:64, :64] + ((high_mid + both[64:128, :64]) + small)
    lower = jnp.concatenate([gram[:32, :32], gram[32:, :32], gram[32:, 32:]], axis=0)
    packed = jnp.concatenate([lower[24 * part : 24 * part + 24] for part in range(4)], axis=1)
    for copy in range(4):
        gram_ref[copy] = packed


def inverse_factor(gram):
    lanes = lax.broadcasted_iota(jnp.int32, (8, 128), 1)
    subs = lax.broadcasted_iota(jnp.int32, (8, 128), 0)
    blocks = []
    for b in range(8):
        eye = jnp.where(lanes == subs + (64 + 8 * b), 1.0, 0.0).astype(jnp.float32)
        left = jnp.concatenate([gram[8 * b : 8 * b + 8], jnp.zeros((8, 64), jnp.float32)], axis=1)
        blocks.append(left + eye)
    done = []
    for panel in range(8):
        cols = []
        for j in range(8):
            k = 8 * panel + j
            cols.append([jnp.broadcast_to(block[:, k : k + 1], (8, 128)) for block in blocks[panel:]])
        for j in range(8):
            row = jnp.broadcast_to(blocks[panel][j : j + 1, :], (8, 128))
            pivot = jnp.broadcast_to(cols[j][0][j : j + 1, :], (8, 128))
            done.append((row * lax.rsqrt(pivot))[:1, 64:])
            inverse = 1.0 / pivot
            factors = [col * inverse for col in cols[j]]
            factors[0] = jnp.where(subs > j, factors[0], 0.0)
            for later in range(j + 1, 8):
                entry = jnp.broadcast_to(cols[later][0][j : j + 1, :], (8, 128))
                cols[later] = [col - f * entry for col, f in zip(cols[later], factors)]
            for i, f in enumerate(factors):
                blocks[panel + i] = blocks[panel + i] - f * row
    return jnp.concatenate(done, axis=0)


def finish_kernel(parts_ref, mixed_ref, out_ref, result, sems, *, total_feat):
    packed = parts_ref[0]
    for index in range(1, parts_ref.shape[0]):
        packed = packed + parts_ref[index]
    packed = packed / total_feat
    lower = jnp.concatenate([packed[:, 32 * part : 32 * part + 32] for part in range(4)], axis=0)
    gram = jnp.concatenate(
        [
            jnp.concatenate([lower[:32], lower[32:64].T], axis=1),
            jnp.concatenate([lower[32:64], lower[64:]], axis=1),
        ],
        axis=0,
    )
    inverse = inverse_factor(gram)
    width = result.shape[1] // CHUNKS
    copies = []
    for c in range(CHUNKS):
        span = slice(width * c, width * c + width)
        result[:, span] = exact_dot(inverse, mixed_ref[:, span])
        copy = pltpu.make_async_copy(result.at[:, span], out_ref.at[:, span], sems.at[c])
        copy.start()
        copies.append(copy)
    for copy in copies:
        copy.wait()


def fold_kernel(parts_ref, out_ref):
    total = (parts_ref[0] + parts_ref[1]) + (parts_ref[2] + parts_ref[3])
    for index in range(8):
        out_ref[index] = total


def across(value, pairs):
    return lax.ppermute(value, "y", pairs + [(b, a) for a, b in pairs])


def per_device(basis, stream):
    start, batches = basis[0], stream[0]
    rank, width = start.shape
    total_feat = float(width * 32)
    mega = 1 << 20
    dma = pltpu.SemaphoreType.DMA
    held_start = pltpu.VMEM(start.shape, jnp.float32)
    held_stream = pltpu.VMEM(batches.shape, jnp.bfloat16)
    quarter = (4, 16, width // 4)

    arrived = lax.all_to_all(start.reshape(4, 16, width), "x", 0, 0)
    (feat,) = kernel_call(
        products_kernel,
        (IN_VMEM, IN_HBM),
        [((256, 128), IN_VMEM)],
        (start, batches),
        700 * mega,
        8 * mega,
        (held_stream, dma((CHUNKS,))),
        FIRST_LIMIT,
    )
    feat = feat + lax.ppermute(feat, "core", SWAP)
    pieces, feat = kernel_call(
        pack_kernel,
        (IN_VMEM,) * 3,
        [(quarter, IN_HBM), ((256, 128), IN_VMEM)],
        (arrived, feat, lax.ppermute(feat, "zl", SWAP)),
        mega,
        2 * mega,
        (pltpu.VMEM(quarter, jnp.float32), dma((4,))),
    )
    pieces = lax.all_to_all(pieces, "zh", 0, 0)
    pieces, feat = kernel_call(
        turn_kernel,
        (IN_VMEM,) * 3,
        [(quarter, IN_HBM), ((256, 128), IN_VMEM)],
        (pieces, feat, across(feat, PAIRS[0])),
        mega,
        2 * mega,
        (pltpu.VMEM(quarter[1:], jnp.float32), dma((4,))),
    )
    pieces = lax.all_to_all(pieces, "zh", 0, 0)
    chunk, feat = kernel_call(
        unpack_kernel,
        (IN_VMEM,) * 3,
        [((4,) + quarter, IN_HBM), ((256, 128), IN_VMEM)],
        (pieces, feat, across(feat, PAIRS[1])),
        mega,
        2 * mega,
        (dma((4,)),),
        53500 << 10,
    )
    average = lax.all_to_all(chunk, "x", 0, 0)
    (delta,) = kernel_call(
        functools.partial(
            delta_kernel, inv_scale=total_feat**-0.5, step_size=LEARN_RATE / batches.shape[1]
        ),
        (IN_VMEM, IN_VMEM, IN_VMEM, IN_HBM),
        [((rank, width), IN_VMEM)],
        (feat, across(feat, PAIRS[2]), start, batches),
        700 * mega,
        8 * mega,
        (held_stream, dma((CHUNKS,))),
        DELTA_LIMIT,
    )
    mixed, gram = kernel_call(
        gram_kernel,
        (IN_VMEM, IN_VMEM),
        [((rank, width), IN_VMEM), ((4, 24, 128), IN_VMEM)],
        (average, delta),
        400 * mega,
        3 * mega,
        (),
        GRAM_LIMIT,
    )
    gram = lax.all_to_all(gram, ("zl", "core"), 0, 0)
    (gram,) = kernel_call(fold_kernel, (IN_VMEM,), [((8, 24, 128), IN_VMEM)], (gram,), mega, mega)
    parts = lax.all_to_all(gram, "y", 0, 0)
    (result,) = kernel_call(
        functools.partial(finish_kernel, total_feat=total_feat),
        (IN_VMEM, IN_VMEM),
        [((rank, width), IN_HBM)],
        (parts, mixed),
        400 * mega,
        3 * mega,
        (held_start, dma((CHUNKS,))),
        FINISH_LIMIT,
    )
    return result[None]


def solution(mesh):
    fine = Mesh(mesh.devices.reshape(SIZES), AXES)
    placed = (P(REP, None, FEAT), P(REP, None, None, FEAT))
    return jax.shard_map(
        per_device, mesh=fine, in_specs=placed, out_specs=P(REP, None, FEAT), check_vma=False
    )
```

```python
import functools

import jax
import jax.numpy as jnp
from jax import lax
from jax.experimental import pallas as pl
from jax.experimental.pallas import tpu as pltpu
from jax.sharding import Mesh, PartitionSpec as P

REP = ("x", "zh")
FEAT = ("zl", "y", "core")
AXES = REP + FEAT
SIZES = (4, 4, 2, 8, 2)
LEARN_RATE = 0.5
HIGHEST = lax.Precision.HIGHEST
SWAP = [(0, 1), (1, 0)]
PAIRS = (
    [(0, 1), (2, 3), (4, 5), (6, 7)],
    [(1, 2), (3, 4), (5, 6), (7, 0)],
    [(1, 6), (2, 5), (0, 3), (4, 7)],
)
PLAIN = ((1,), (0,))
ON_ROWS = ((0,), (0,))
ON_COLS = ((1,), (1,))


def dot(left, right, dims, precision=HIGHEST):
    return lax.dot_general(
        left, right, (dims, ((), ())), precision=precision, preferred_element_type=jnp.float32
    )


def split3(value):
    high = value.astype(jnp.bfloat16)
    rest = value - high.astype(jnp.float32)
    middle = rest.astype(jnp.bfloat16)
    low = (rest - middle.astype(jnp.float32)).astype(jnp.bfloat16)
    return high, middle, low


def exact_dot(left, right):
    high, middle, low = split3(left)
    left = jnp.concatenate([high, high, high, middle, middle, low], axis=1)
    high, middle, low = split3(right)
    right = jnp.concatenate([high, middle, low, high, middle, high], axis=0)
    return dot(left, right, PLAIN, None)


IN_HBM = pl.BlockSpec(memory_space=pltpu.HBM)
IN_VMEM = pl.BlockSpec(memory_space=pltpu.VMEM)
CHUNKS = 4
LARGE = 55000 << 10
FIRST_LIMIT = 53000 << 10
DELTA_LIMIT = 52000 << 10
GRAM_LIMIT = 50000 << 10
FINISH_LIMIT = 53000 << 10


def kernel_call(body, ins, outs, args, flops, moved, scratch=(), limit=20 << 20):
    return pl.pallas_call(
        body,
        out_shape=tuple(f32(*shape) for shape, _ in outs),
        in_specs=list(ins),
        out_specs=tuple(space for _, space in outs),
        scratch_shapes=list(scratch),
        cost_estimate=pl.CostEstimate(flops=flops, bytes_accessed=moved, transcendentals=0),
        compiler_params=pltpu.CompilerParams(vmem_limit_bytes=limit),
    )(*args)


def fetch(pairs, sems):
    copies = [
        pltpu.make_async_copy(source, target, sems.at[index])
        for index, (source, target) in enumerate(pairs)
    ]
    for copy in copies:
        copy.start()
    return copies


def f32(*shape):
    return jax.ShapeDtypeStruct(shape, jnp.float32)


def products_kernel(start_ref, stream_ref, out_ref, stream_vmem, sems):
    width = start_ref.shape[1] // CHUNKS
    spans = [slice(width * c, width * c + width) for c in range(CHUNKS)]
    copies = fetch([(stream_ref.at[:, :, s], stream_vmem.at[:, :, s]) for s in spans], sems)
    both = None
    for c, span in enumerate(spans):
        copies[c].wait()
        first = stream_vmem[0, :, span]
        rows = jnp.concatenate([first, stream_vmem[1, :, span]], axis=0)
        right = jnp.concatenate(split3(start_ref[:, span]) + (first,), axis=0)
        part = dot(rows, right, ON_COLS, None)
        both = part if both is None else both + part
    onto = both[:, :64] + (both[:, 64:128] + both[:, 128:192])
    out_ref[:128] = jnp.concatenate([onto[:128], onto[128:]], axis=1)
    out_ref[128:] = both[128:, 192:]


def pack_kernel(received_ref, feat_ref, other_ref, out_ref, sum_ref, total, sems):
    sum_ref[...] = feat_ref[...] + other_ref[...]
    width = total.shape[2]
    copies = []
    for piece in range(4):
        cols = slice(width * piece, width * piece + width)
        total[piece] = (received_ref[0, :, cols] + received_ref[1, :, cols]) + (
            received_ref[2, :, cols] + received_ref[3, :, cols]
        )
        copy = pltpu.make_async_copy(total.at[piece], out_ref.at[piece], sems.at[piece])
        copy.start()
        copies.append(copy)
    for copy in copies:
        copy.wait()


def turn_kernel(received_ref, feat_ref, other_ref, out_ref, sum_ref, total, sems):
    sum_ref[...] = feat_ref[...] + other_ref[...]
    part = (received_ref[0] + received_ref[1]) + (received_ref[2] + received_ref[3])
    total[...] = part * (1.0 / 16.0)
    for copy in fetch([(total, out_ref.at[piece]) for piece in range(4)], sems):
        copy.wait()


def unpack_kernel(received_ref, feat_ref, other_ref, out_ref, sum_ref, sems):
    copies = fetch([(received_ref, out_ref.at[x]) for x in range(4)], sems)
    sum_ref[...] = feat_ref[...] + other_ref[...]
    for copy in copies:
        copy.wait()


def delta_kernel(
    feat_ref, other_ref, start_ref, stream_ref, out_ref, stream_vmem, sems,
    *, inv_scale, step_size
):
    width = out_ref.shape[1] // CHUNKS
    spans = [slice(width * c, width * c + width) for c in range(CHUNKS)]
    arriving = fetch([(stream_ref.at[:, :, s], stream_vmem.at[:, :, s]) for s in spans], sems)
    rank = start_ref.shape[0]
    index = lax.broadcasted_iota(jnp.int32, (rank, rank), 0)
    eye = jnp.where(index == lax.broadcasted_iota(jnp.int32, (rank, rank), 1), 1.0, 0.0)
    onto0 = feat_ref[:128, :64] + other_ref[:128, :64]
    onto1 = feat_ref[:128, 64:] + other_ref[:128, 64:]
    cross = feat_ref[128:] + other_ref[128:]
    proj0 = onto0 * inv_scale
    cov0 = dot(proj0, proj0, ON_ROWS)
    proj1 = (dot(onto1, eye - step_size * cov0, PLAIN) + step_size * dot(cross, proj0, PLAIN)) * inv_scale
    cov1 = dot(proj1, proj1, ON_ROWS)
    mix_b = step_size * (step_size * dot(cov1, cov0, PLAIN) - cov0 - cov1)
    turned0 = proj0.T
    mix_0 = step_size * (turned0 - step_size * dot(cov1, turned0, PLAIN))
    mix_1 = step_size * proj1.T
    left = jnp.concatenate([mix_b, mix_b, mix_b, mix_0, mix_1], axis=1)
    left = jnp.concatenate(split3(left), axis=0)
    for c, span in enumerate(spans):
        arriving[c].wait()
        right = split3(start_ref[:, span]) + (stream_vmem[0, :, span], stream_vmem[1, :, span])
        three = dot(left, jnp.concatenate(right, axis=0), PLAIN, None)
        out_ref[:, span] = three[:64] + (three[64:128] + three[128:])


def gram_kernel(average_ref, delta_ref, mixed_ref, gram_ref):
    parts, pieces, rows, width = average_ref.shape
    for part in range(parts):
        for piece in range(pieces):
            place = (slice(rows * part, rows * part + rows), slice(width * piece, width * piece + width))
            mixed_ref[place] = average_ref[part, piece] + delta_ref[place]
    stacked = jnp.concatenate(split3(mixed_ref[...]), axis=0)
    both = dot(stacked, stacked, ON_COLS, None)
    high_mid = both[:64, 64:128]
    high_low = both[:64, 128:192]
    small = both[64:128, 64:128] + (high_low + both[128:192, :64])
    gram = both[:64, :64] + ((high_mid + both[64:128, :64]) + small)
    lower = jnp.concatenate([gram[:32, :32], gram[32:, :32], gram[32:, 32:]], axis=0)
    packed = jnp.concatenate([lower[24 * part : 24 * part + 24] for part in range(4)], axis=1)
    gram_ref[...] = packed


def inverse_factor(gram):
    lanes = lax.broadcasted_iota(jnp.int32, (8, 128), 1)
    subs = lax.broadcasted_iota(jnp.int32, (8, 128), 0)
    blocks = []
    for b in range(8):
        eye = jnp.where(lanes == subs + (64 + 8 * b), 1.0, 0.0).astype(jnp.float32)
        left = jnp.concatenate([gram[8 * b : 8 * b + 8], jnp.zeros((8, 64), jnp.float32)], axis=1)
        blocks.append(left + eye)
    done = []
    for panel in range(8):
        cols = []
        for j in range(8):
            k = 8 * panel + j
            cols.append([jnp.broadcast_to(block[:, k : k + 1], (8, 128)) for block in blocks[panel:]])
        for j in range(8):
            row = jnp.broadcast_to(blocks[panel][j : j + 1, :], (8, 128))
            pivot = jnp.broadcast_to(cols[j][0][j : j + 1, :], (8, 128))
            done.append((row * lax.rsqrt(pivot))[:1, 64:])
            inverse = 1.0 / pivot
            factors = [col * inverse for col in cols[j]]
            factors[0] = jnp.where(subs > j, factors[0], 0.0)
            for later in range(j + 1, 8):
                entry = jnp.broadcast_to(cols[later][0][j : j + 1, :], (8, 128))
                cols[later] = [col - f * entry for col, f in zip(cols[later], factors)]
            for i, f in enumerate(factors):
                blocks[panel + i] = blocks[panel + i] - f * row
    return jnp.concatenate(done, axis=0)


def finish_kernel(parts_ref, mixed_ref, out_ref, result, sems, *, total_feat):
    packed = parts_ref[0]
    for index in range(1, parts_ref.shape[0]):
        packed = packed + parts_ref[index]
    packed = packed / total_feat
    lower = jnp.concatenate([packed[:, 32 * part : 32 * part + 32] for part in range(4)], axis=0)
    gram = jnp.concatenate(
        [
            jnp.concatenate([lower[:32], lower[32:64].T], axis=1),
            jnp.concatenate([lower[32:64], lower[64:]], axis=1),
        ],
        axis=0,
    )
    inverse = inverse_factor(gram)
    width = result.shape[1] // CHUNKS
    copies = []
    for c in range(CHUNKS):
        span = slice(width * c, width * c + width)
        result[:, span] = exact_dot(inverse, mixed_ref[:, span])
        copy = pltpu.make_async_copy(result.at[:, span], out_ref.at[:, span], sems.at[c])
        copy.start()
        copies.append(copy)
    for copy in copies:
        copy.wait()


def fold_kernel(left_ref, right_ref, out_ref):
    total = left_ref[...] + right_ref[...]
    for index in range(16):
        out_ref[index] = total


def across(value, pairs):
    return lax.ppermute(value, "y", pairs + [(b, a) for a, b in pairs])


def per_device(basis, stream):
    start, batches = basis[0], stream[0]
    rank, width = start.shape
    total_feat = float(width * 32)
    mega = 1 << 20
    dma = pltpu.SemaphoreType.DMA
    held_start = pltpu.VMEM(start.shape, jnp.float32)
    held_stream = pltpu.VMEM(batches.shape, jnp.bfloat16)
    quarter = (4, 16, width // 4)

    arrived = lax.all_to_all(start.reshape(4, 16, width), "x", 0, 0)
    (feat,) = kernel_call(
        products_kernel,
        (IN_VMEM, IN_HBM),
        [((256, 128), IN_VMEM)],
        (start, batches),
        700 * mega,
        8 * mega,
        (held_stream, dma((CHUNKS,))),
        FIRST_LIMIT,
    )
    feat = feat + lax.ppermute(feat, "core", SWAP)
    pieces, feat = kernel_call(
        pack_kernel,
        (IN_VMEM,) * 3,
        [(quarter, IN_HBM), ((256, 128), IN_VMEM)],
        (arrived, feat, lax.ppermute(feat, "zl", SWAP)),
        mega,
        2 * mega,
        (pltpu.VMEM(quarter, jnp.float32), dma((4,))),
    )
    pieces = lax.all_to_all(pieces, "zh", 0, 0)
    pieces, feat = kernel_call(
        turn_kernel,
        (IN_VMEM,) * 3,
        [(quarter, IN_HBM), ((256, 128), IN_VMEM)],
        (pieces, feat, across(feat, PAIRS[0])),
        mega,
        2 * mega,
        (pltpu.VMEM(quarter[1:], jnp.float32), dma((4,))),
    )
    pieces = lax.all_to_all(pieces, "zh", 0, 0)
    chunk, feat = kernel_call(
        unpack_kernel,
        (IN_VMEM,) * 3,
        [((4,) + quarter, IN_HBM), ((256, 128), IN_VMEM)],
        (pieces, feat, across(feat, PAIRS[1])),
        mega,
        2 * mega,
        (dma((4,)),),
        53500 << 10,
    )
    average = lax.all_to_all(chunk, "x", 0, 0)
    (delta,) = kernel_call(
        functools.partial(
            delta_kernel, inv_scale=total_feat**-0.5, step_size=LEARN_RATE / batches.shape[1]
        ),
        (IN_VMEM, IN_VMEM, IN_VMEM, IN_HBM),
        [((rank, width), IN_VMEM)],
        (feat, across(feat, PAIRS[2]), start, batches),
        700 * mega,
        8 * mega,
        (held_stream, dma((CHUNKS,))),
        DELTA_LIMIT,
    )
    mixed, gram = kernel_call(
        gram_kernel,
        (IN_VMEM, IN_VMEM),
        [((rank, width), IN_VMEM), ((24, 128), IN_VMEM)],
        (average, delta),
        400 * mega,
        3 * mega,
        (),
        GRAM_LIMIT,
    )
    (gram,) = kernel_call(
        fold_kernel,
        (IN_VMEM, IN_VMEM),
        [((16, 24, 128), IN_VMEM)],
        (gram, lax.ppermute(gram, "core", SWAP)),
        mega,
        mega,
    )
    parts = lax.all_to_all(gram, ("zl", "y"), 0, 0)
    (result,) = kernel_call(
        functools.partial(finish_kernel, total_feat=total_feat),
        (IN_VMEM, IN_VMEM),
        [((rank, width), IN_HBM)],
        (parts, mixed),
        400 * mega,
        3 * mega,
        (held_start, dma((CHUNKS,))),
        FINISH_LIMIT,
    )
    return result[None]


def solution(mesh):
    fine = Mesh(mesh.devices.reshape(SIZES), AXES)
    placed = (P(REP, None, FEAT), P(REP, None, None, FEAT))
    return jax.shard_map(
        per_device, mesh=fine, in_specs=placed, out_specs=P(REP, None, FEAT), check_vma=False
    )
```

```python
import functools

import jax
import jax.numpy as jnp
from jax import lax
from jax.experimental import pallas as pl
from jax.experimental.pallas import tpu as pltpu
from jax.sharding import Mesh, PartitionSpec as P

REP = ("x", "zh")
FEAT = ("zl", "y", "core")
AXES = REP + FEAT
SIZES = (4, 4, 2, 8, 2)
LEARN_RATE = 0.5
HIGHEST = lax.Precision.HIGHEST
SWAP = [(0, 1), (1, 0)]
PAIRS = (
    [(0, 1), (2, 3), (4, 5), (6, 7)],
    [(1, 2), (3, 4), (5, 6), (7, 0)],
    [(1, 6), (2, 5), (0, 3), (4, 7)],
)
PLAIN = ((1,), (0,))
ON_ROWS = ((0,), (0,))
ON_COLS = ((1,), (1,))


def dot(left, right, dims, precision=HIGHEST):
    return lax.dot_general(
        left, right, (dims, ((), ())), precision=precision, preferred_element_type=jnp.float32
    )


def split3(value):
    high = value.astype(jnp.bfloat16)
    rest = value - high.astype(jnp.float32)
    middle = rest.astype(jnp.bfloat16)
    low = (rest - middle.astype(jnp.float32)).astype(jnp.bfloat16)
    return high, middle, low


def exact_dot(left, right):
    high, middle, low = split3(left)
    left = jnp.concatenate([high, high, high, middle, middle, low], axis=1)
    high, middle, low = split3(right)
    right = jnp.concatenate([high, middle, low, high, middle, high], axis=0)
    return dot(left, right, PLAIN, None)


IN_HBM = pl.BlockSpec(memory_space=pltpu.HBM)
IN_VMEM = pl.BlockSpec(memory_space=pltpu.VMEM)
CHUNKS = 4
LARGE = 55000 << 10
FIRST_LIMIT = 53000 << 10
DELTA_LIMIT = 52000 << 10
GRAM_LIMIT = 50000 << 10
FINISH_LIMIT = 53000 << 10


def kernel_call(body, ins, outs, args, flops, moved, scratch=(), limit=20 << 20):
    return pl.pallas_call(
        body,
        out_shape=tuple(f32(*shape) for shape, _ in outs),
        in_specs=list(ins),
        out_specs=tuple(space for _, space in outs),
        scratch_shapes=list(scratch),
        cost_estimate=pl.CostEstimate(flops=flops, bytes_accessed=moved, transcendentals=0),
        compiler_params=pltpu.CompilerParams(vmem_limit_bytes=limit),
    )(*args)


def fetch(pairs, sems):
    copies = [
        pltpu.make_async_copy(source, target, sems.at[index])
        for index, (source, target) in enumerate(pairs)
    ]
    for copy in copies:
        copy.start()
    return copies


def f32(*shape):
    return jax.ShapeDtypeStruct(shape, jnp.float32)


def products_kernel(start_ref, stream_ref, out_ref, stream_vmem, sems):
    width = start_ref.shape[1] // CHUNKS
    spans = [slice(width * c, width * c + width) for c in range(CHUNKS)]
    copies = fetch([(stream_ref.at[:, :, s], stream_vmem.at[:, :, s]) for s in spans], sems)
    both = None
    for c, span in enumerate(spans):
        copies[c].wait()
        first = stream_vmem[0, :, span]
        rows = jnp.concatenate([first, stream_vmem[1, :, span]], axis=0)
        right = jnp.concatenate(split3(start_ref[:, span]) + (first,), axis=0)
        part = dot(rows, right, ON_COLS, None)
        both = part if both is None else both + part
    onto = both[:, :64] + (both[:, 64:128] + both[:, 128:192])
    out_ref[:128] = jnp.concatenate([onto[:128], onto[128:]], axis=1)
    out_ref[128:] = both[128:, 192:]


def pack_kernel(received_ref, feat_ref, other_ref, out_ref, sum_ref, total, sems):
    sum_ref[...] = feat_ref[...] + other_ref[...]
    width = total.shape[2]
    copies = []
    for piece in range(4):
        cols = slice(width * piece, width * piece + width)
        total[piece] = (received_ref[0, :, cols] + received_ref[1, :, cols]) + (
            received_ref[2, :, cols] + received_ref[3, :, cols]
        )
        copy = pltpu.make_async_copy(total.at[piece], out_ref.at[piece], sems.at[piece])
        copy.start()
        copies.append(copy)
    for copy in copies:
        copy.wait()


def turn_kernel(received_ref, feat_ref, other_ref, out_ref, sum_ref, total, sems):
    sum_ref[...] = feat_ref[...] + other_ref[...]
    part = (received_ref[0] + received_ref[1]) + (received_ref[2] + received_ref[3])
    total[...] = part * (1.0 / 16.0)
    for copy in fetch([(total, out_ref.at[piece]) for piece in range(4)], sems):
        copy.wait()


def unpack_kernel(received_ref, feat_ref, other_ref, out_ref, sum_ref, sems):
    copies = fetch([(received_ref, out_ref.at[x]) for x in range(4)], sems)
    sum_ref[...] = feat_ref[...] + other_ref[...]
    for copy in copies:
        copy.wait()


def delta_kernel(
    feat_ref, other_ref, start_ref, stream_ref, out_ref, stream_vmem, sems,
    *, inv_scale, step_size
):
    width = out_ref.shape[1] // CHUNKS
    spans = [slice(width * c, width * c + width) for c in range(CHUNKS)]
    arriving = fetch([(stream_ref.at[:, :, s], stream_vmem.at[:, :, s]) for s in spans], sems)
    rank = start_ref.shape[0]
    index = lax.broadcasted_iota(jnp.int32, (rank, rank), 0)
    eye = jnp.where(index == lax.broadcasted_iota(jnp.int32, (rank, rank), 1), 1.0, 0.0)
    onto0 = feat_ref[:128, :64] + other_ref[:128, :64]
    onto1 = feat_ref[:128, 64:] + other_ref[:128, 64:]
    cross = feat_ref[128:] + other_ref[128:]
    proj0 = onto0 * inv_scale
    turned0 = proj0.T
    cov0 = exact_dot(turned0, proj0)
    onto_cross = jnp.concatenate([onto1, cross], axis=1)
    proj1 = inv_scale * exact_dot(
        onto_cross, jnp.concatenate([eye - step_size * cov0, step_size * proj0], axis=0)
    )
    turned1 = proj1.T
    cov1 = exact_dot(turned1, proj1)
    both = step_size * exact_dot(cov1, jnp.concatenate([turned0, cov0], axis=1))
    mix_b = step_size * (both[:, 128:] - cov0 - cov1)
    mix_0 = step_size * (turned0 - both[:, :128])
    mix_1 = step_size * turned1
    left = jnp.concatenate([mix_b, mix_b, mix_b, mix_0, mix_1], axis=1)
    left = jnp.concatenate(split3(left), axis=0)
    for c, span in enumerate(spans):
        arriving[c].wait()
        right = split3(start_ref[:, span]) + (stream_vmem[0, :, span], stream_vmem[1, :, span])
        three = dot(left, jnp.concatenate(right, axis=0), PLAIN, None)
        out_ref[:, span] = three[:64] + (three[64:128] + three[128:])


def gram_kernel(average_ref, delta_ref, mixed_ref, gram_ref):
    parts, pieces, rows, width = average_ref.shape
    for part in range(parts):
        for piece in range(pieces):
            place = (slice(rows * part, rows * part + rows), slice(width * piece, width * piece + width))
            mixed_ref[place] = average_ref[part, piece] + delta_ref[place]
    stacked = jnp.concatenate(split3(mixed_ref[...]), axis=0)
    both = dot(stacked, stacked, ON_COLS, None)
    high_mid = both[:64, 64:128]
    high_low = both[:64, 128:192]
    small = both[64:128, 64:128] + (high_low + both[128:192, :64])
    gram = both[:64, :64] + ((high_mid + both[64:128, :64]) + small)
    lower = jnp.concatenate([gram[:32, :32], gram[32:, :32], gram[32:, 32:]], axis=0)
    packed = jnp.concatenate([lower[24 * part : 24 * part + 24] for part in range(4)], axis=1)
    gram_ref[...] = packed


def inverse_factor(gram):
    lanes = lax.broadcasted_iota(jnp.int32, (8, 128), 1)
    subs = lax.broadcasted_iota(jnp.int32, (8, 128), 0)
    blocks = []
    for b in range(8):
        eye = jnp.where(lanes == subs + (64 + 8 * b), 1.0, 0.0).astype(jnp.float32)
        left = jnp.concatenate([gram[8 * b : 8 * b + 8], jnp.zeros((8, 64), jnp.float32)], axis=1)
        blocks.append(left + eye)
    done = []
    for panel in range(8):
        cols = []
        for j in range(8):
            k = 8 * panel + j
            cols.append([jnp.broadcast_to(block[:, k : k + 1], (8, 128)) for block in blocks[panel:]])
        for j in range(8):
            row = jnp.broadcast_to(blocks[panel][j : j + 1, :], (8, 128))
            pivot = jnp.broadcast_to(cols[j][0][j : j + 1, :], (8, 128))
            done.append((row * lax.rsqrt(pivot))[:1, 64:])
            inverse = 1.0 / pivot
            factors = [col * inverse for col in cols[j]]
            factors[0] = jnp.where(subs > j, factors[0], 0.0)
            for later in range(j + 1, 8):
                entry = jnp.broadcast_to(cols[later][0][j : j + 1, :], (8, 128))
                cols[later] = [col - f * entry for col, f in zip(cols[later], factors)]
            for i, f in enumerate(factors):
                blocks[panel + i] = blocks[panel + i] - f * row
    return jnp.concatenate(done, axis=0)


def finish_kernel(parts_ref, mixed_ref, out_ref, result, sems, *, total_feat):
    packed = parts_ref[0]
    for index in range(1, parts_ref.shape[0]):
        packed = packed + parts_ref[index]
    packed = packed / total_feat
    lower = jnp.concatenate([packed[:, 32 * part : 32 * part + 32] for part in range(4)], axis=0)
    gram = jnp.concatenate(
        [
            jnp.concatenate([lower[:32], lower[32:64].T], axis=1),
            jnp.concatenate([lower[32:64], lower[64:]], axis=1),
        ],
        axis=0,
    )
    inverse = inverse_factor(gram)
    width = result.shape[1] // CHUNKS
    copies = []
    for c in range(CHUNKS):
        span = slice(width * c, width * c + width)
        result[:, span] = exact_dot(inverse, mixed_ref[:, span])
        copy = pltpu.make_async_copy(result.at[:, span], out_ref.at[:, span], sems.at[c])
        copy.start()
        copies.append(copy)
    for copy in copies:
        copy.wait()


def fold_kernel(left_ref, right_ref, out_ref):
    total = left_ref[...] + right_ref[...]
    for index in range(16):
        out_ref[index] = total


def across(value, pairs):
    return lax.ppermute(value, "y", pairs + [(b, a) for a, b in pairs])


def per_device(basis, stream):
    start, batches = basis[0], stream[0]
    rank, width = start.shape
    total_feat = float(width * 32)
    mega = 1 << 20
    dma = pltpu.SemaphoreType.DMA
    held_start = pltpu.VMEM(start.shape, jnp.float32)
    held_stream = pltpu.VMEM(batches.shape, jnp.bfloat16)
    quarter = (4, 16, width // 4)

    arrived = lax.all_to_all(start.reshape(4, 16, width), "x", 0, 0)
    (feat,) = kernel_call(
        products_kernel,
        (IN_VMEM, IN_HBM),
        [((256, 128), IN_VMEM)],
        (start, batches),
        700 * mega,
        8 * mega,
        (held_stream, dma((CHUNKS,))),
        FIRST_LIMIT,
    )
    feat = feat + lax.ppermute(feat, "core", SWAP)
    pieces, feat = kernel_call(
        pack_kernel,
        (IN_VMEM,) * 3,
        [(quarter, IN_HBM), ((256, 128), IN_VMEM)],
        (arrived, feat, lax.ppermute(feat, "zl", SWAP)),
        mega,
        2 * mega,
        (pltpu.VMEM(quarter, jnp.float32), dma((4,))),
    )
    pieces = lax.all_to_all(pieces, "zh", 0, 0)
    pieces, feat = kernel_call(
        turn_kernel,
        (IN_VMEM,) * 3,
        [(quarter, IN_HBM), ((256, 128), IN_VMEM)],
        (pieces, feat, across(feat, PAIRS[0])),
        mega,
        2 * mega,
        (pltpu.VMEM(quarter[1:], jnp.float32), dma((4,))),
    )
    pieces = lax.all_to_all(pieces, "zh", 0, 0)
    chunk, feat = kernel_call(
        unpack_kernel,
        (IN_VMEM,) * 3,
        [((4,) + quarter, IN_HBM), ((256, 128), IN_VMEM)],
        (pieces, feat, across(feat, PAIRS[1])),
        mega,
        2 * mega,
        (dma((4,)),),
        53500 << 10,
    )
    average = lax.all_to_all(chunk, "x", 0, 0)
    (delta,) = kernel_call(
        functools.partial(
            delta_kernel, inv_scale=total_feat**-0.5, step_size=LEARN_RATE / batches.shape[1]
        ),
        (IN_VMEM, IN_VMEM, IN_VMEM, IN_HBM),
        [((rank, width), IN_VMEM)],
        (feat, across(feat, PAIRS[2]), start, batches),
        700 * mega,
        8 * mega,
        (held_stream, dma((CHUNKS,))),
        DELTA_LIMIT,
    )
    mixed, gram = kernel_call(
        gram_kernel,
        (IN_VMEM, IN_VMEM),
        [((rank, width), IN_VMEM), ((24, 128), IN_VMEM)],
        (average, delta),
        400 * mega,
        3 * mega,
        (),
        GRAM_LIMIT,
    )
    (gram,) = kernel_call(
        fold_kernel,
        (IN_VMEM, IN_VMEM),
        [((16, 24, 128), IN_VMEM)],
        (gram, lax.ppermute(gram, "core", SWAP)),
        mega,
        mega,
    )
    parts = lax.all_to_all(gram, ("zl", "y"), 0, 0)
    (result,) = kernel_call(
        functools.partial(finish_kernel, total_feat=total_feat),
        (IN_VMEM, IN_VMEM),
        [((rank, width), IN_HBM)],
        (parts, mixed),
        400 * mega,
        3 * mega,
        (held_start, dma((CHUNKS,))),
        FINISH_LIMIT,
    )
    return result[None]


def solution(mesh):
    fine = Mesh(mesh.devices.reshape(SIZES), AXES)
    placed = (P(REP, None, FEAT), P(REP, None, None, FEAT))
    return jax.shard_map(
        per_device, mesh=fine, in_specs=placed, out_specs=P(REP, None, FEAT), check_vma=False
    )
```

```python
import functools

import jax
import jax.numpy as jnp
from jax import lax
from jax.experimental import pallas as pl
from jax.experimental.pallas import tpu as pltpu
from jax.sharding import Mesh, PartitionSpec as P

REP = ("x", "zh")
FEAT = ("zl", "y", "core")
AXES = REP + FEAT
SIZES = (4, 4, 2, 8, 2)
LEARN_RATE = 0.5
HIGHEST = lax.Precision.HIGHEST
SWAP = [(0, 1), (1, 0)]
PAIRS = (
    [(0, 1), (2, 3), (4, 5), (6, 7)],
    [(1, 2), (3, 4), (5, 6), (7, 0)],
    [(1, 6), (2, 5), (0, 3), (4, 7)],
)
PLAIN = ((1,), (0,))
ON_ROWS = ((0,), (0,))
ON_COLS = ((1,), (1,))


def dot(left, right, dims, precision=HIGHEST):
    return lax.dot_general(
        left, right, (dims, ((), ())), precision=precision, preferred_element_type=jnp.float32
    )


def split3(value):
    high = value.astype(jnp.bfloat16)
    rest = value - high.astype(jnp.float32)
    middle = rest.astype(jnp.bfloat16)
    low = (rest - middle.astype(jnp.float32)).astype(jnp.bfloat16)
    return high, middle, low


def exact_dot(left, right):
    high, middle, low = split3(left)
    left = jnp.concatenate([high, high, high, middle, middle, low], axis=1)
    high, middle, low = split3(right)
    right = jnp.concatenate([high, middle, low, high, middle, high], axis=0)
    return dot(left, right, PLAIN, None)


IN_HBM = pl.BlockSpec(memory_space=pltpu.HBM)
IN_VMEM = pl.BlockSpec(memory_space=pltpu.VMEM)
CHUNKS = 4
LARGE = 55000 << 10
FIRST_LIMIT = 53000 << 10
DELTA_LIMIT = 52000 << 10
GRAM_LIMIT = 50000 << 10
FINISH_LIMIT = 53000 << 10


def kernel_call(body, ins, outs, args, flops, moved, scratch=(), limit=20 << 20):
    return pl.pallas_call(
        body,
        out_shape=tuple(f32(*shape) for shape, _ in outs),
        in_specs=list(ins),
        out_specs=tuple(space for _, space in outs),
        scratch_shapes=list(scratch),
        cost_estimate=pl.CostEstimate(flops=flops, bytes_accessed=moved, transcendentals=0),
        compiler_params=pltpu.CompilerParams(vmem_limit_bytes=limit),
    )(*args)


def fetch(pairs, sems):
    copies = [
        pltpu.make_async_copy(source, target, sems.at[index])
        for index, (source, target) in enumerate(pairs)
    ]
    for copy in copies:
        copy.start()
    return copies


def f32(*shape):
    return jax.ShapeDtypeStruct(shape, jnp.float32)


def products_kernel(start_ref, stream_ref, out_ref, stream_vmem, sems):
    width = start_ref.shape[1] // CHUNKS
    spans = [slice(width * c, width * c + width) for c in range(CHUNKS)]
    copies = fetch([(stream_ref.at[:, :, s], stream_vmem.at[:, :, s]) for s in spans], sems)
    both = None
    for c, span in enumerate(spans):
        copies[c].wait()
        first = stream_vmem[0, :, span]
        rows = jnp.concatenate([first, stream_vmem[1, :, span]], axis=0)
        right = jnp.concatenate(split3(start_ref[:, span]) + (first,), axis=0)
        part = dot(rows, right, ON_COLS, None)
        both = part if both is None else both + part
    onto = both[:, :64] + (both[:, 64:128] + both[:, 128:192])
    out_ref[:128] = jnp.concatenate([onto[:128], onto[128:]], axis=1)
    out_ref[128:] = both[128:, 192:]


def pack_kernel(received_ref, feat_ref, other_ref, out_ref, sum_ref, total, sems):
    sum_ref[...] = feat_ref[...] + other_ref[...]
    width = total.shape[2]
    copies = []
    for piece in range(4):
        cols = slice(width * piece, width * piece + width)
        total[piece] = (received_ref[0, :, cols] + received_ref[1, :, cols]) + (
            received_ref[2, :, cols] + received_ref[3, :, cols]
        )
        copy = pltpu.make_async_copy(total.at[piece], out_ref.at[piece], sems.at[piece])
        copy.start()
        copies.append(copy)
    for copy in copies:
        copy.wait()


def turn_kernel(received_ref, feat_ref, other_ref, out_ref, sum_ref, total, sems):
    sum_ref[...] = feat_ref[...] + other_ref[...]
    part = (received_ref[0] + received_ref[1]) + (received_ref[2] + received_ref[3])
    total[...] = part * (1.0 / 16.0)
    for copy in fetch([(total, out_ref.at[piece]) for piece in range(4)], sems):
        copy.wait()


def unpack_kernel(received_ref, feat_ref, other_ref, out_ref, sum_ref, sems):
    copies = fetch([(received_ref, out_ref.at[x]) for x in range(4)], sems)
    sum_ref[...] = feat_ref[...] + other_ref[...]
    for copy in copies:
        copy.wait()


def delta_kernel(
    feat_ref, other_ref, start_ref, stream_ref, out_ref, stream_vmem, sems,
    *, inv_scale, step_size
):
    width = out_ref.shape[1] // CHUNKS
    spans = [slice(width * c, width * c + width) for c in range(CHUNKS)]
    arriving = fetch([(stream_ref.at[:, :, s], stream_vmem.at[:, :, s]) for s in spans], sems)
    rank = start_ref.shape[0]
    index = lax.broadcasted_iota(jnp.int32, (rank, rank), 0)
    eye = jnp.where(index == lax.broadcasted_iota(jnp.int32, (rank, rank), 1), 1.0, 0.0)
    onto0 = feat_ref[:128, :64] + other_ref[:128, :64]
    onto1 = feat_ref[:128, 64:] + other_ref[:128, 64:]
    cross = feat_ref[128:] + other_ref[128:]
    proj0 = onto0 * inv_scale
    cov0 = dot(proj0, proj0, ON_ROWS)
    proj1 = (dot(onto1, eye - step_size * cov0, PLAIN) + step_size * dot(cross, proj0, PLAIN)) * inv_scale
    cov1 = dot(proj1, proj1, ON_ROWS)
    mix_b = step_size * (step_size * dot(cov1, cov0, PLAIN) - cov0 - cov1)
    turned0 = proj0.T
    mix_0 = step_size * (turned0 - step_size * dot(cov1, turned0, PLAIN))
    mix_1 = step_size * proj1.T
    left = jnp.concatenate([mix_b, mix_b, mix_b, mix_0, mix_1], axis=1)
    left = jnp.concatenate(split3(left), axis=0)
    for c, span in enumerate(spans):
        arriving[c].wait()
        right = split3(start_ref[:, span]) + (stream_vmem[0, :, span], stream_vmem[1, :, span])
        three = dot(left, jnp.concatenate(right, axis=0), PLAIN, None)
        out_ref[:, span] = three[:64] + (three[64:128] + three[128:])


def gram_kernel(average_ref, delta_ref, mixed_ref, gram_ref):
    parts, pieces, rows, width = average_ref.shape
    for part in range(parts):
        for piece in range(pieces):
            place = (slice(rows * part, rows * part + rows), slice(width * piece, width * piece + width))
            mixed_ref[place] = average_ref[part, piece] + delta_ref[place]
    stacked = jnp.concatenate(split3(mixed_ref[...]), axis=0)
    both = dot(stacked, stacked, ON_COLS, None)
    high_mid = both[:64, 64:128]
    high_low = both[:64, 128:192]
    small = both[64:128, 64:128] + (high_low + both[128:192, :64])
    gram = both[:64, :64] + ((high_mid + both[64:128, :64]) + small)
    lower = jnp.concatenate([gram[:32, :32], gram[32:, :32], gram[32:, 32:]], axis=0)
    packed = jnp.concatenate([lower[24 * part : 24 * part + 24] for part in range(4)], axis=1)
    gram_ref[...] = packed


def inverse_factor(gram):
    lanes = lax.broadcasted_iota(jnp.int32, (8, 128), 1)
    subs = lax.broadcasted_iota(jnp.int32, (8, 128), 0)
    blocks = []
    for b in range(8):
        eye = jnp.where(lanes == subs + (64 + 8 * b), 1.0, 0.0).astype(jnp.float32)
        left = jnp.concatenate([gram[8 * b : 8 * b + 8], jnp.zeros((8, 64), jnp.float32)], axis=1)
        blocks.append(left + eye)
    done = []
    for panel in range(8):
        cols = []
        for j in range(8):
            k = 8 * panel + j
            cols.append([jnp.broadcast_to(block[:, k : k + 1], (8, 128)) for block in blocks[panel:]])
        for j in range(8):
            row = jnp.broadcast_to(blocks[panel][j : j + 1, :], (8, 128))
            pivot = jnp.broadcast_to(cols[j][0][j : j + 1, :], (8, 128))
            done.append((row * lax.rsqrt(pivot))[:1, 64:])
            inverse = 1.0 / pivot
            factors = [col * inverse for col in cols[j]]
            factors[0] = jnp.where(subs > j, factors[0], 0.0)
            for later in range(j + 1, 8):
                entry = jnp.broadcast_to(cols[later][0][j : j + 1, :], (8, 128))
                cols[later] = [col - f * entry for col, f in zip(cols[later], factors)]
            for i, f in enumerate(factors):
                blocks[panel + i] = blocks[panel + i] - f * row
    return jnp.concatenate(done, axis=0)


def finish_kernel(parts_ref, mixed_ref, out_ref, result, sems, *, total_feat):
    packed = parts_ref[0]
    for index in range(1, parts_ref.shape[0]):
        packed = packed + parts_ref[index]
    packed = packed / total_feat
    lower = jnp.concatenate([packed[:, 32 * part : 32 * part + 32] for part in range(4)], axis=0)
    gram = jnp.concatenate(
        [
            jnp.concatenate([lower[:32], lower[32:64].T], axis=1),
            jnp.concatenate([lower[32:64], lower[64:]], axis=1),
        ],
        axis=0,
    )
    inverse = inverse_factor(gram)
    left = jnp.concatenate(split3(jnp.concatenate([inverse] * 3, axis=1)), axis=0)
    width = result.shape[1] // CHUNKS
    copies = []
    for c in range(CHUNKS):
        span = slice(width * c, width * c + width)
        right = jnp.concatenate(split3(mixed_ref[:, span]), axis=0)
        three = dot(left, right, PLAIN, None)
        result[:, span] = three[:64] + (three[64:128] + three[128:])
        copy = pltpu.make_async_copy(result.at[:, span], out_ref.at[:, span], sems.at[c])
        copy.start()
        copies.append(copy)
    for copy in copies:
        copy.wait()


def fold_kernel(left_ref, right_ref, out_ref):
    total = left_ref[...] + right_ref[...]
    for index in range(16):
        out_ref[index] = total


def across(value, pairs):
    return lax.ppermute(value, "y", pairs + [(b, a) for a, b in pairs])


def per_device(basis, stream):
    start, batches = basis[0], stream[0]
    rank, width = start.shape
    total_feat = float(width * 32)
    mega = 1 << 20
    dma = pltpu.SemaphoreType.DMA
    held_start = pltpu.VMEM(start.shape, jnp.float32)
    held_stream = pltpu.VMEM(batches.shape, jnp.bfloat16)
    quarter = (4, 16, width // 4)

    arrived = lax.all_to_all(start.reshape(4, 16, width), "x", 0, 0)
    (feat,) = kernel_call(
        products_kernel,
        (IN_VMEM, IN_HBM),
        [((256, 128), IN_VMEM)],
        (start, batches),
        700 * mega,
        8 * mega,
        (held_stream, dma((CHUNKS,))),
        FIRST_LIMIT,
    )
    feat = feat + lax.ppermute(feat, "core", SWAP)
    pieces, feat = kernel_call(
        pack_kernel,
        (IN_VMEM,) * 3,
        [(quarter, IN_HBM), ((256, 128), IN_VMEM)],
        (arrived, feat, lax.ppermute(feat, "zl", SWAP)),
        mega,
        2 * mega,
        (pltpu.VMEM(quarter, jnp.float32), dma((4,))),
    )
    pieces = lax.all_to_all(pieces, "zh", 0, 0)
    pieces, feat = kernel_call(
        turn_kernel,
        (IN_VMEM,) * 3,
        [(quarter, IN_HBM), ((256, 128), IN_VMEM)],
        (pieces, feat, across(feat, PAIRS[0])),
        mega,
        2 * mega,
        (pltpu.VMEM(quarter[1:], jnp.float32), dma((4,))),
    )
    pieces = lax.all_to_all(pieces, "zh", 0, 0)
    chunk, feat = kernel_call(
        unpack_kernel,
        (IN_VMEM,) * 3,
        [((4,) + quarter, IN_HBM), ((256, 128), IN_VMEM)],
        (pieces, feat, across(feat, PAIRS[1])),
        mega,
        2 * mega,
        (dma((4,)),),
        53500 << 10,
    )
    average = lax.all_to_all(chunk, "x", 0, 0)
    (delta,) = kernel_call(
        functools.partial(
            delta_kernel, inv_scale=total_feat**-0.5, step_size=LEARN_RATE / batches.shape[1]
        ),
        (IN_VMEM, IN_VMEM, IN_VMEM, IN_HBM),
        [((rank, width), IN_VMEM)],
        (feat, across(feat, PAIRS[2]), start, batches),
        700 * mega,
        8 * mega,
        (held_stream, dma((CHUNKS,))),
        DELTA_LIMIT,
    )
    mixed, gram = kernel_call(
        gram_kernel,
        (IN_VMEM, IN_VMEM),
        [((rank, width), IN_VMEM), ((24, 128), IN_VMEM)],
        (average, delta),
        400 * mega,
        3 * mega,
        (),
        GRAM_LIMIT,
    )
    (gram,) = kernel_call(
        fold_kernel,
        (IN_VMEM, IN_VMEM),
        [((16, 24, 128), IN_VMEM)],
        (gram, lax.ppermute(gram, "core", SWAP)),
        mega,
        mega,
    )
    parts = lax.all_to_all(gram, ("zl", "y"), 0, 0)
    (result,) = kernel_call(
        functools.partial(finish_kernel, total_feat=total_feat),
        (IN_VMEM, IN_VMEM),
        [((rank, width), IN_HBM)],
        (parts, mixed),
        400 * mega,
        3 * mega,
        (held_start, dma((CHUNKS,))),
        FINISH_LIMIT,
    )
    return result[None]


def solution(mesh):
    fine = Mesh(mesh.devices.reshape(SIZES), AXES)
    placed = (P(REP, None, FEAT), P(REP, None, None, FEAT))
    return jax.shard_map(
        per_device, mesh=fine, in_specs=placed, out_specs=P(REP, None, FEAT), check_vma=False
    )
```
